256 devices in a mesh: row: 16 (over z, core), col: 16 (over y, x).
Axes of the slice: x: 4, y: 4, z: 8, core: 2. Of those that a mesh axis runs over, the one named last changes fastest.
Arguments:
- covariance: float32 [8, 16, 8, 16, 128, 128], P(None, 'row', None, 'col'), as said below
Outputs:
- panel_factor: float32 [8, 16, 6, 128, 128], P(None, 'row')
- trailing: float32 [8, 16, 8, 16, 128, 128], P(None, 'row', None, 'col')
- logdet_mean: float32 [], replicated
Inputs may be any that keep to these rules, and one draw needn't show every extreme that they name: `covariance`: the 16384 x 16384 matrix A assembled from the tiles is symmetric and positive definite, every eigenvalue 0.5 or more.
All inputs are finite; a program needn't handle non-finite values.
Results may differ from the reference program's by a relative error of at most 0.0054.
Values may be sent and summed in bfloat16 or wider, within the bound.
No kernel may reach another device: no remote copies, remote signals or barrier semaphores. Data moves between devices by JAX's collectives and lax.ppermute only.
A program may use at most 128 MiB of HBM per device.

```python
import jax
import jax.numpy as jnp
from jax import lax

N = 16384
NB = 128
STEPS = 6
ROW_TILES = 8
COL_TILES = 8
N_ROW = 16
N_COL = 16


def draw_covariance(key, part):
    key = jax.random.fold_in(key, 7)
    key_points, key_scales, key_nugget = jax.random.split(key, 3)
    points = jax.random.uniform(key_points, (N, 3), jnp.float32)
    scales = jnp.exp(jax.random.uniform(key_scales, (N,), jnp.float32, 0.0, 0.5 * jnp.log(10.0)))
    nugget = jax.random.uniform(key_nugget, (N,), jnp.float32, 0.5, 1.5)
    length_scale = 3.8 * float(N) ** (-1.0 / 3.0)
    squared = (points[:, None, 0] - points[None, :, 0]) ** 2
    squared = squared + (points[:, None, 1] - points[None, :, 1]) ** 2
    squared = squared + (points[:, None, 2] - points[None, :, 2]) ** 2
    distance = jnp.sqrt(squared)
    kernel = scales[:, None] * scales[None, :] * jnp.exp(-distance / length_scale)
    row_place = jnp.arange(N)[:, None]
    col_place = jnp.arange(N)[None, :]
    assembled = kernel + jnp.where(row_place == col_place, nugget[:, None], 0.0)
    blocked = assembled.reshape(ROW_TILES, N_ROW, NB, COL_TILES, N_COL, NB)
    return blocked.transpose(0, 1, 3, 4, 2, 5).astype(jnp.float32)


def setup_inputs(seed: int = 0) -> dict:
    key_of = jax.random.split(jax.random.key(seed), 2)
    covariance = draw_covariance(jax.random.fold_in(key_of[1], 71), 0)
    return {"covariance": covariance}


def reference(covariance):
    matrix = covariance.transpose(0, 1, 4, 2, 3, 5).reshape(N, N)
    panels = []
    log_terms = jnp.zeros((), jnp.float32)
    for section in range(STEPS):
        start = section * NB
        column = matrix[:, start:start + NB]
        factor_tile = jnp.linalg.cholesky(column[start:start + NB])
        below_rows = column[start + NB:]
        solved = jax.scipy.linalg.solve_triangular(factor_tile, below_rows.T, lower=True).T
        column_panel = jnp.concatenate([jnp.zeros((start, NB), jnp.float32), factor_tile, solved], axis=0)
        panels.append(column_panel)
        log_terms = log_terms + jnp.sum(jnp.log(jnp.diagonal(factor_tile)))
        rounded = lax.optimization_barrier(column_panel.astype(jnp.bfloat16)).astype(jnp.float32)
        matrix = matrix - jnp.dot(rounded.astype(jnp.float32), rounded.T.astype(jnp.float32), precision=lax.Precision.HIGHEST, preferred_element_type=jnp.float32)
    stacked = jnp.stack(panels, axis=0).reshape(STEPS, ROW_TILES, N_ROW, NB, NB)
    panel_factor = stacked.transpose(1, 2, 0, 3, 4)
    trailing = matrix.reshape(ROW_TILES, N_ROW, NB, COL_TILES, N_COL, NB).transpose(0, 1, 3, 4, 2, 5)
    logdet_mean = 2.0 * log_terms / (STEPS * NB)
    return (panel_factor, trailing, logdet_mean)
```

```python
import jax
import jax.numpy as jnp
from jax import lax
from jax.experimental import pallas as pl
from jax.experimental.pallas import tpu as pltpu
from jax.sharding import PartitionSpec as P

STEPS = 6
NB = 128
LT = 8
SB = 16
UPPER = STEPS * (STEPS + 1) // 2


def split2(x):
    hi = x.astype(jnp.bfloat16)
    lo = (x - hi.astype(jnp.float32)).astype(jnp.bfloat16)
    return hi, lo

def chain_kernel(d_ref, ub_ref, linv_ref, logdet_ref, w_ref):
    ub_ref[...] = jnp.zeros_like(ub_ref)
    eye = (lax.broadcasted_iota(jnp.int32, (NB, NB), 0) == lax.broadcasted_iota(jnp.int32, (NB, NB), 1)).astype(jnp.float32)
    rows16 = lax.broadcasted_iota(jnp.int32, (SB, NB), 0)
    def step(k, logs):
        kk = pl.multiple_of(k * NB, NB)
        left = ub_ref[:, pl.ds(kk, NB)]
        for t in range(STEPS):
            j = lax.rem(k + t, STEPS)
            jj = pl.multiple_of(j * NB, NB)
            low, high = jnp.minimum(k, j), jnp.maximum(k, j)
            place = low * STEPS - low * (low - 1) // 2 + high - low
            upd = lax.dot_general(left, ub_ref[:, pl.ds(jj, NB)], (((0,), (0,)), ((), ())), preferred_element_type=jnp.float32)
            w_ref[:, t * NB:(t + 1) * NB] = d_ref[:, place].reshape(NB, NB) - upd
        w_ref[:, STEPS * NB:] = eye
        for s in range(NB // SB):
            r0 = s * SB
            nl = STEPS + 1
            R = [w_ref[r0:r0 + SB, t * NB:(t + 1) * NB] for t in range(nl)]
            cols = [jnp.broadcast_to(R[0][:, r0 + p:r0 + p + 1], (SB, NB)) for p in range(SB)]
            for p in range(SB):
                inv = lax.rsqrt(jnp.broadcast_to(cols[p][p:p + 1, :], (SB, NB)))
                l = cols[p] * inv
                below = rows16 > p
                lm = jnp.where(below, l, 0.0)
                for q in range(p + 1, SB):
                    cols[q] = cols[q] - lm * jnp.broadcast_to(l[q:q + 1, :], (SB, NB))
                for t in range(nl):
                    u = jnp.broadcast_to(R[t][p:p + 1, :], (SB, NB)) * inv
                    R[t] = jnp.where(rows16 == p, u, R[t] - lm * u)
            for t in range(nl):
                w_ref[r0:r0 + SB, t * NB:(t + 1) * NB] = R[t]
            if s < NB // SB - 1:
                X = jnp.concatenate(R, axis=1)
                xhi, xlo = split2(X)
                r1 = r0 + SB
                lh, ll = xhi[:, :NB], xlo[:, :NB]
                L = jnp.concatenate([lh, lh, ll], axis=0)
                Rr = jnp.concatenate([xhi, xlo, xhi], axis=0)
                upd = lax.dot_general(L, Rr, (((0,), (0,)), ((), ())), preferred_element_type=jnp.float32)
                w_ref[r1:, :] = w_ref[r1:, :] - upd[r1:, :]
        tri = lax.broadcasted_iota(jnp.int32, (NB, NB), 0) <= lax.broadcasted_iota(jnp.int32, (NB, NB), 1)
        for t in range(STEPS):
            j = lax.rem(k + t, STEPS)
            jj = pl.multiple_of(j * NB, NB)
            keep = k + t < STEPS
            x = w_ref[:, t * NB:(t + 1) * NB]
            if t == 0:
                x = jnp.where(tri, x, 0.0)
                logs = logs + jnp.sum(jnp.log(jnp.sum(x * eye, axis=0, keepdims=True)), axis=1, keepdims=True)
            else:
                x = jnp.where(keep, x, 0.0)
            ub_ref[pl.ds(kk, NB), pl.ds(jj, NB)] = x.astype(jnp.bfloat16)
        linv_ref[k] = w_ref[:, STEPS * NB:]
        return logs
    logs = lax.fori_loop(0, STEPS, step, jnp.zeros((1, 1), jnp.float32))
    logdet_ref[...] = logs * (2.0 / (STEPS * NB))

def chain(d):
    return pl.pallas_call(
        chain_kernel,
        out_shape=(jax.ShapeDtypeStruct((STEPS * NB, STEPS * NB), jnp.bfloat16),
                   jax.ShapeDtypeStruct((STEPS, NB, NB), jnp.float32),
                   jax.ShapeDtypeStruct((1, 1), jnp.float32)),
        in_specs=[pl.BlockSpec(memory_space=pltpu.VMEM)],
        out_specs=(pl.BlockSpec(memory_space=pltpu.VMEM),) * 3,
        scratch_shapes=[pltpu.VMEM((NB, (STEPS + 1) * NB), jnp.float32)],
        compiler_params=pltpu.CompilerParams(vmem_limit_bytes=48 * 2**20),
        name="chain",
    )(d)


def finish_kernel(place_ref, a_hbm, rp_ref, cp_ref, ub_ref, linv_ref, pf_hbm, tr_hbm, a_ref, p_ref, b_ref, q_ref, in_sem, p_sem, t_sem):
    row = place_ref[0]
    col = place_ref[1]
    loads = [pltpu.make_async_copy(a_hbm.at[l], a_ref.at[l], in_sem.at[l]) for l in range(LT)]
    for c in loads:
        c.start()
    ri = lax.broadcasted_iota(jnp.int32, (NB, NB), 0)
    ci = lax.broadcasted_iota(jnp.int32, (NB, NB), 1)
    stores = []
    for k in range(STEPS):
        lhi, llo = split2(linv_ref[k])
        s = jnp.concatenate([rp_ref[l, k] for l in range(LT)], axis=0)
        if k:
            s = s - jnp.dot(b_ref[:, :k * NB], ub_ref[:k * NB, k * NB:(k + 1) * NB], preferred_element_type=jnp.float32)
        shi, slo = split2(s)
        p = lax.dot_general(jnp.concatenate([shi, shi, slo], axis=1), jnp.concatenate([lhi, llo, lhi], axis=1),
                            (((1,), (1,)), ((), ())), preferred_element_type=jnp.float32)
        keep = jnp.where(row == k, ri - ci, row - k) >= 0
        first = jnp.where(keep, p[:NB], 0.0)
        p_ref[0, k] = first
        for l in range(1, LT):
            p_ref[l, k] = p[l * NB:(l + 1) * NB]
        b_ref[:NB, k * NB:(k + 1) * NB] = first.astype(jnp.bfloat16)
        b_ref[NB:, k * NB:(k + 1) * NB] = p[NB:].astype(jnp.bfloat16)
        st = pltpu.make_async_copy(p_ref.at[:, k], pf_hbm.at[:, k], p_sem.at[k])
        st.start()
        stores.append(st)
        s = jnp.concatenate([cp_ref[k, m].astype(jnp.float32) for m in range(LT)], axis=1)
        if k:
            s = s - lax.dot_general(ub_ref[:k * NB, k * NB:(k + 1) * NB], q_ref[:k * NB, :], (((0,), (0,)), ((), ())),
                                    preferred_element_type=jnp.float32)
        shi, slo = split2(s)
        q = jnp.dot(jnp.concatenate([lhi, lhi, llo], axis=1), jnp.concatenate([shi, slo, shi], axis=0),
                    preferred_element_type=jnp.float32)
        keep = jnp.where(col == k, ci - ri, col - k) >= 0
        q_ref[k * NB:(k + 1) * NB, :NB] = jnp.where(keep, q[:, :NB], 0.0).astype(jnp.bfloat16)
        q_ref[k * NB:(k + 1) * NB, NB:] = q[:, NB:].astype(jnp.bfloat16)
    for l in range(LT):
        loads[l].wait()
        upd = jnp.dot(b_ref[l * NB:(l + 1) * NB, :], q_ref[...], preferred_element_type=jnp.float32)
        for m in range(LT):
            a_ref[l, m] = a_ref[l, m] - upd[:, m * NB:(m + 1) * NB]
        st = pltpu.make_async_copy(a_ref.at[l], tr_hbm.at[l], t_sem.at[l])
        st.start()
        stores.append(st)
    for st in stores:
        st.wait()

def finish(place, a, rp, cp, ub, linv):
    vm = pl.BlockSpec(memory_space=pltpu.VMEM)
    hb = pl.BlockSpec(memory_space=pl.ANY)
    return pl.pallas_call(
        finish_kernel,
        out_shape=(jax.ShapeDtypeStruct((LT, STEPS, NB, NB), jnp.float32),
                   jax.ShapeDtypeStruct((LT, LT, NB, NB), jnp.float32)),
        in_specs=[pl.BlockSpec(memory_space=pltpu.SMEM), hb, vm, vm, vm, vm],
        out_specs=(hb, hb),
        scratch_shapes=[pltpu.VMEM((LT, LT, NB, NB), jnp.float32), pltpu.VMEM((LT, STEPS, NB, NB), jnp.float32),
                        pltpu.VMEM((LT * NB, STEPS * NB), jnp.bfloat16), pltpu.VMEM((STEPS * NB, LT * NB), jnp.bfloat16),
                        pltpu.SemaphoreType.DMA((LT,)), pltpu.SemaphoreType.DMA((STEPS,)), pltpu.SemaphoreType.DMA((LT,))],
        compiler_params=pltpu.CompilerParams(vmem_limit_bytes=48 * 2**20),
        name="finish",
    )(place, a, rp, cp, ub, linv)


def diagonal_block(tile):
    slabs = lax.all_to_all(tile, "row", 0, 0, tiled=True).reshape(16, 8, NB)[:STEPS]
    spread = jnp.broadcast_to(slabs[None], (16, STEPS, 8, NB)).reshape(16 * STEPS * 8, NB)
    slabs = lax.all_to_all(spread, "col", 0, 0, tiled=True).reshape(16, STEPS, 8, NB)
    upper = jnp.stack([slabs[q, p] for p in range(STEPS) for q in range(p, STEPS)])
    spread = jnp.broadcast_to(upper[None], (16,) + upper.shape).reshape(-1, NB)
    return lax.all_to_all(spread, "row", 0, 0, tiled=True).reshape(16, UPPER, 8, NB)


def shards(covariance):
    matrix = covariance[:, 0, :, 0]
    corner = diagonal_block(matrix[0, 0])
    across = lax.all_gather(matrix[0], "row", axis=0, tiled=False)[:STEPS]
    down = lax.all_gather(matrix[:, 0], "col", axis=1, tiled=False)[:, :STEPS]
    ub, linv, logdet = chain(corner)
    place = jnp.stack([lax.axis_index("row"), lax.axis_index("col")]).astype(jnp.int32)
    panel, trailing = finish(place, matrix, down, across, ub, linv)
    return panel[:, None], trailing[:, None, :, None], logdet[0, 0]


def solution(mesh):
    in_specs = (P(None, "row", None, "col", None, None),)
    out_specs = (P(None, "row", None, None, None), P(None, "row", None, "col", None, None), P())
    return jax.shard_map(shards, mesh=mesh, in_specs=in_specs, out_specs=out_specs, check_vma=False)
```

```python
import jax
import jax.numpy as jnp
from jax import lax
from jax.experimental import pallas as pl
from jax.experimental.pallas import tpu as pltpu
from jax.sharding import PartitionSpec as P

STEPS = 6
NB = 128
LT = 8
SB = 16
HALF = 12
SHIFT = 13.0


def split2(x):
    hi = x.astype(jnp.bfloat16)
    lo = (x - hi.astype(jnp.float32)).astype(jnp.bfloat16)
    return hi, lo

def chain_kernel(place_ref, mine_ref, other_ref, ub_ref, linv_ref, logdet_ref, w_ref, d_ref):
    core = lax.rem(place_ref[0], 2)
    for n in range(HALF):
        d_ref[core, n] = mine_ref[:, n].reshape(NB, NB)
        d_ref[1 - core, n] = other_ref[:, n].reshape(NB, NB)
    ub_ref[...] = jnp.zeros_like(ub_ref)
    eye = (lax.broadcasted_iota(jnp.int32, (NB, NB), 0) == lax.broadcasted_iota(jnp.int32, (NB, NB), 1)).astype(jnp.float32)
    rows16 = lax.broadcasted_iota(jnp.int32, (SB, NB), 0)
    def step(k, logs):
        kk = pl.multiple_of(k * NB, NB)
        left = ub_ref[:, pl.ds(kk, NB)]
        for t in range(STEPS):
            j = lax.rem(k + t, STEPS)
            jj = pl.multiple_of(j * NB, NB)
            low, high = jnp.minimum(k, j), jnp.maximum(k, j)
            pair = low // 2
            place = pair * STEPS - pair * (pair - 1) + high - 2 * pair
            upd = lax.dot_general(left, ub_ref[:, pl.ds(jj, NB)], (((0,), (0,)), ((), ())), preferred_element_type=jnp.float32)
            w_ref[:, t * NB:(t + 1) * NB] = d_ref[lax.rem(low, 2), place] - upd
        w_ref[:, STEPS * NB:] = eye
        for s in range(NB // SB):
            r0 = s * SB
            nl = STEPS + 1
            R = [w_ref[r0:r0 + SB, t * NB:(t + 1) * NB] for t in range(nl)]
            cols = [jnp.broadcast_to(R[0][:, r0 + p:r0 + p + 1], (SB, NB)) for p in range(SB)]
            for p in range(SB):
                inv = lax.rsqrt(jnp.broadcast_to(cols[p][p:p + 1, :], (SB, NB)))
                l = cols[p] * inv
                below = rows16 > p
                lm = jnp.where(below, l, 0.0)
                for q in range(p + 1, SB):
                    cols[q] = cols[q] - lm * jnp.broadcast_to(l[q:q + 1, :], (SB, NB))
                for t in range(nl):
                    u = jnp.broadcast_to(R[t][p:p + 1, :], (SB, NB)) * inv
                    R[t] = jnp.where(rows16 == p, u, R[t] - lm * u)
            for t in range(nl):
                w_ref[r0:r0 + SB, t * NB:(t + 1) * NB] = R[t]
            if s < NB // SB - 1:
                X = jnp.concatenate(R, axis=1)
                xhi, xlo = split2(X)
                r1 = r0 + SB
                lh, ll = xhi[:, :NB], xlo[:, :NB]
                L = jnp.concatenate([lh, lh, ll], axis=0)
                Rr = jnp.concatenate([xhi, xlo, xhi], axis=0)
                upd = lax.dot_general(L, Rr, (((0,), (0,)), ((), ())), preferred_element_type=jnp.float32)
                w_ref[r1:, :] = w_ref[r1:, :] - upd[r1:, :]
        tri = lax.broadcasted_iota(jnp.int32, (NB, NB), 0) <= lax.broadcasted_iota(jnp.int32, (NB, NB), 1)
        for t in range(STEPS):
            j = lax.rem(k + t, STEPS)
            jj = pl.multiple_of(j * NB, NB)
            keep = k + t < STEPS
            x = w_ref[:, t * NB:(t + 1) * NB]
            if t == 0:
                x = jnp.where(tri, x, 0.0)
                logs = logs + jnp.sum(jnp.log(jnp.sum(x * eye, axis=0, keepdims=True)), axis=1, keepdims=True)
            else:
                x = jnp.where(keep, x, 0.0)
            ub_ref[pl.ds(kk, NB), pl.ds(jj, NB)] = x.astype(jnp.bfloat16)
        linv_ref[k] = w_ref[:, STEPS * NB:]
        return logs
    logs = lax.fori_loop(0, STEPS, step, jnp.zeros((1, 1), jnp.float32))
    logdet_ref[...] = logs * (2.0 / (STEPS * NB))

def chain(place, mine, other):
    return pl.pallas_call(
        chain_kernel,
        out_shape=(jax.ShapeDtypeStruct((STEPS * NB, STEPS * NB), jnp.bfloat16),
                   jax.ShapeDtypeStruct((STEPS, NB, NB), jnp.float32),
                   jax.ShapeDtypeStruct((1, 1), jnp.float32)),
        in_specs=[pl.BlockSpec(memory_space=pltpu.SMEM)] + [pl.BlockSpec(memory_space=pltpu.VMEM)] * 2,
        out_specs=(pl.BlockSpec(memory_space=pltpu.VMEM),) * 3,
        scratch_shapes=[pltpu.VMEM((NB, (STEPS + 1) * NB), jnp.float32), pltpu.VMEM((2, HALF, NB, NB), jnp.float32)],
        compiler_params=pltpu.CompilerParams(vmem_limit_bytes=48 * 2**20),
        cost_estimate=pl.CostEstimate(flops=30_000_000_000, bytes_accessed=4 * 2**20, transcendentals=0),
        name="chain",
    )(place, mine, other)


def finish_kernel(place_ref, a_hbm, rp_ref, cp_hbm, ub_ref, linv_ref, pf_hbm, tr_hbm, a_ref, cp_ref, p_ref, b_ref, q_ref, in_sem, c_sem, p_sem, t_sem):
    row = place_ref[0]
    col = place_ref[1]
    loads = [pltpu.make_async_copy(a_hbm.at[l], a_ref.at[l], in_sem.at[l]) for l in range(LT)]
    tops = [pltpu.make_async_copy(cp_hbm.at[k], cp_ref.at[k], c_sem.at[k]) for k in range(STEPS)]
    for c in tops + loads:
        c.start()
    ri = lax.broadcasted_iota(jnp.int32, (NB, NB), 0)
    ci = lax.broadcasted_iota(jnp.int32, (NB, NB), 1)
    stores = []
    for k in range(STEPS):
        lhi, llo = split2(linv_ref[k])
        s = jnp.concatenate([rp_ref[:, k, l].reshape(NB, NB) for l in range(LT)], axis=0)
        if k:
            s = s - jnp.dot(b_ref[:, :k * NB], ub_ref[:k * NB, k * NB:(k + 1) * NB], preferred_element_type=jnp.float32)
        shi, slo = split2(s)
        p = lax.dot_general(jnp.concatenate([shi, shi, slo], axis=1), jnp.concatenate([lhi, llo, lhi], axis=1),
                            (((1,), (1,)), ((), ())), preferred_element_type=jnp.float32)
        keep = jnp.where(row == k, ri - ci, row - k) >= 0
        first = jnp.where(keep, p[:NB], 0.0)
        p_ref[0, k] = first
        for l in range(1, LT):
            p_ref[l, k] = p[l * NB:(l + 1) * NB]
        b_ref[:NB, k * NB:(k + 1) * NB] = first.astype(jnp.bfloat16)
        b_ref[NB:, k * NB:(k + 1) * NB] = p[NB:].astype(jnp.bfloat16)
        st = pltpu.make_async_copy(p_ref.at[:, k], pf_hbm.at[:, k], p_sem.at[k])
        st.start()
        stores.append(st)
        tops[k].wait()
        s = jnp.concatenate([cp_ref[k, m] for m in range(LT)], axis=1)
        if k:
            s = s - lax.dot_general(ub_ref[:k * NB, k * NB:(k + 1) * NB], q_ref[:k * NB, :], (((0,), (0,)), ((), ())),
                                    preferred_element_type=jnp.float32)
        shi, slo = split2(s)
        q = jnp.dot(jnp.concatenate([lhi, lhi, llo], axis=1), jnp.concatenate([shi, slo, shi], axis=0),
                    preferred_element_type=jnp.float32)
        keep = jnp.where(col == k, ci - ri, col - k) >= 0
        q_ref[k * NB:(k + 1) * NB, :NB] = jnp.where(keep, q[:, :NB], 0.0).astype(jnp.bfloat16)
        q_ref[k * NB:(k + 1) * NB, NB:] = q[:, NB:].astype(jnp.bfloat16)
    for l in range(LT):
        loads[l].wait()
        upd = jnp.dot(b_ref[l * NB:(l + 1) * NB, :], q_ref[...], preferred_element_type=jnp.float32)
        for m in range(LT):
            a_ref[l, m] = a_ref[l, m] - upd[:, m * NB:(m + 1) * NB]
        st = pltpu.make_async_copy(a_ref.at[l], tr_hbm.at[l], t_sem.at[l])
        st.start()
        stores.append(st)
    for st in stores:
        st.wait()

def finish(place, a, rp, cp, ub, linv):
    vm = pl.BlockSpec(memory_space=pltpu.VMEM)
    hb = pl.BlockSpec(memory_space=pl.ANY)
    return pl.pallas_call(
        finish_kernel,
        out_shape=(jax.ShapeDtypeStruct((LT, STEPS, NB, NB), jnp.float32),
                   jax.ShapeDtypeStruct((LT, LT, NB, NB), jnp.float32)),
        in_specs=[pl.BlockSpec(memory_space=pltpu.SMEM), hb, vm, hb, vm, vm],
        out_specs=(hb, hb),
        scratch_shapes=[pltpu.VMEM((LT, LT, NB, NB), jnp.float32), pltpu.VMEM((STEPS, LT, NB, NB), jnp.float32),
                        pltpu.VMEM((LT, STEPS, NB, NB), jnp.float32),
                        pltpu.VMEM((LT * NB, STEPS * NB), jnp.bfloat16), pltpu.VMEM((STEPS * NB, LT * NB), jnp.bfloat16),
                        pltpu.SemaphoreType.DMA((LT,)), pltpu.SemaphoreType.DMA((STEPS,)),
                        pltpu.SemaphoreType.DMA((STEPS,)), pltpu.SemaphoreType.DMA((LT,))],
        compiler_params=pltpu.CompilerParams(vmem_limit_bytes=48 * 2**20),
        name="finish",
    )(place, a, rp, cp, ub, linv)


def spread_kernel(x_ref, o_ref):
    tiles = [x_ref[p, q] for p in range(STEPS // 2) for q in range(2 * p, STEPS)]
    for j in range(16):
        for n, tile in enumerate(tiles):
            o_ref[j, n] = tile


def spread_half(x):
    return pl.pallas_call(
        spread_kernel,
        out_shape=jax.ShapeDtypeStruct((16, HALF, 8, NB), jnp.float32),
        in_specs=[pl.BlockSpec(memory_space=pltpu.VMEM)],
        out_specs=pl.BlockSpec(memory_space=pltpu.VMEM),
        name="spread",
    )(x)


def packed(x):
    top = jnp.maximum(jnp.max(jnp.abs(x)), 1e-30)
    power = jnp.floor(jnp.log2(top))
    body = (x * jnp.exp2(SHIFT - power)).astype(jnp.float16)
    return jnp.concatenate([body, jnp.full((16, NB), power, jnp.float16)], axis=0)


def unpacked(x):
    power = x[:, -16:-15, :1].astype(jnp.float32)
    return x[:, :-16].astype(jnp.float32) * jnp.exp2(power - SHIFT)


def shards(covariance):
    matrix = covariance[:, 0, :, 0]
    row = lax.axis_index("row")
    place = jnp.stack([row, lax.axis_index("col")]).astype(jnp.int32)
    across = lax.all_gather(matrix[0], "row", axis=0, tiled=False)
    first = matrix[:, 0].reshape(LT, 16, 8, NB).transpose(1, 0, 2, 3).reshape(16 * LT * 8, NB)
    slabs = lax.all_to_all(first, "col", 0, 0, tiled=True).reshape(16, LT, 8, NB)[:STEPS]
    sent = jnp.broadcast_to(slabs[None, :, 0], (8, STEPS, 8, NB))
    groups = [[2 * z + c for z in range(8)] for c in range(2)]
    lead = lax.all_to_all(sent, "row", 0, 0, tiled=True, axis_index_groups=groups)
    mine = lax.all_to_all(spread_half(lead), "col", 0, 0, tiled=True)
    other = lax.ppermute(mine, "row", [(i, i ^ 1) for i in range(16)])
    half = packed(slabs.reshape(STEPS * LT * 8, NB))
    half, other = lax.optimization_barrier((half, other))
    down = lax.all_to_all(jnp.broadcast_to(half[None], (16,) + half.shape), "col", 0, 0, tiled=True)
    ub, linv, logdet = chain(place, mine, other)
    down = unpacked(down).reshape(16, STEPS, LT, 8, NB)
    panel, trailing = finish(place, matrix, down, across, ub, linv)
    return panel[:, None], trailing[:, None, :, None], logdet[0, 0]


def solution(mesh):
    in_specs = (P(None, "row", None, "col", None, None),)
    out_specs = (P(None, "row", None, None, None), P(None, "row", None, "col", None, None), P())
    return jax.shard_map(shards, mesh=mesh, in_specs=in_specs, out_specs=out_specs, check_vma=False)
```

```python
import jax
import jax.numpy as jnp
from jax import lax
from jax.experimental import pallas as pl
from jax.experimental.pallas import tpu as pltpu
from jax.sharding import PartitionSpec as P

STEPS = 6
NB = 128
LT = 8
SB = 32
HALF = 12
SHIFT = 13.0


def split2(x):
    hi = x.astype(jnp.bfloat16)
    lo = (x - hi.astype(jnp.float32)).astype(jnp.bfloat16)
    return hi, lo

def chain_kernel(place_ref, mine_ref, other_ref, top_hbm, ub_ref, linv_ref, q_ref, logdet_ref, w_ref, d_ref, top_ref, sem):
    tops = pltpu.make_async_copy(top_hbm.at[pl.ds(0, STEPS)], top_ref, sem)
    tops.start()
    col = place_ref[1]
    core = lax.rem(place_ref[0], 2)
    for n in range(HALF):
        d_ref[core, n] = mine_ref[:, n].reshape(NB, NB)
        d_ref[1 - core, n] = other_ref[:, n].reshape(NB, NB)
    ub_ref[...] = jnp.zeros_like(ub_ref)
    q_ref[...] = jnp.zeros_like(q_ref)
    eye = (lax.broadcasted_iota(jnp.int32, (NB, NB), 0) == lax.broadcasted_iota(jnp.int32, (NB, NB), 1)).astype(jnp.float32)
    rows8 = lax.broadcasted_iota(jnp.int32, (8, NB), 0)
    ri = lax.broadcasted_iota(jnp.int32, (NB, NB), 0)
    ci = lax.broadcasted_iota(jnp.int32, (NB, NB), 1)

    def columns(k):
        kk = pl.multiple_of(k * NB, NB)
        lhi, llo = split2(linv_ref[k])
        x = jnp.concatenate([top_ref[k, m] for m in range(LT)], axis=1)
        x = x - lax.dot_general(ub_ref[:, pl.ds(kk, NB)], q_ref[...], (((0,), (0,)), ((), ())),
                                preferred_element_type=jnp.float32)
        xhi, xlo = split2(x)
        q = jnp.dot(jnp.concatenate([lhi, lhi, llo], axis=1), jnp.concatenate([xhi, xlo, xhi], axis=0),
                    preferred_element_type=jnp.float32)
        keep = jnp.where(col == k, ci - ri, col - k) >= 0
        q_ref[pl.ds(kk, NB), :NB] = jnp.where(keep, q[:, :NB], 0.0).astype(jnp.bfloat16)
        q_ref[pl.ds(kk, NB), NB:] = q[:, NB:].astype(jnp.bfloat16)

    def step(k, logs):
        kk = pl.multiple_of(k * NB, NB)
        left = ub_ref[:, pl.ds(kk, NB)]
        for t in range(STEPS):
            j = lax.rem(k + t, STEPS)
            jj = pl.multiple_of(j * NB, NB)
            low, high = jnp.minimum(k, j), jnp.maximum(k, j)
            pair = low // 2
            place = pair * STEPS - pair * (pair - 1) + high - 2 * pair
            upd = lax.dot_general(left, ub_ref[:, pl.ds(jj, NB)], (((0,), (0,)), ((), ())), preferred_element_type=jnp.float32)
            w_ref[:, t * NB:(t + 1) * NB] = d_ref[lax.rem(low, 2), place] - upd
        w_ref[:, STEPS * NB:] = eye
        if not isinstance(k, int):
            columns(k - 1)
        wide = (0, STEPS)
        for s in range(NB // SB):
            r0 = s * SB
            nb = SB // 8
            R = [[w_ref[r0 + 8 * b:r0 + 8 * b + 8, t * NB:(t + 1) * NB] for b in range(nb)] for t in wide]
            cols = [{b: jnp.broadcast_to(R[0][b][:, r0 + q:r0 + q + 1], (8, NB)) for b in range(q // 8, nb)} for q in range(SB)]
            for p in range(SB):
                pb, pr = p // 8, p % 8
                inv = lax.rsqrt(jnp.broadcast_to(cols[p][pb][pr:pr + 1, :], (8, NB)))
                l = {b: cols[p][b] * inv for b in range(pb, nb)}
                for q in range(p + 1, SB):
                    m = jnp.broadcast_to(l[q // 8][q % 8:q % 8 + 1, :], (8, NB))
                    for b in range(q // 8, nb):
                        cols[q][b] = cols[q][b] - l[b] * m
                for t in range(2):
                    u = jnp.broadcast_to(R[t][pb][pr:pr + 1, :], (8, NB)) * inv
                    if pr < 7:
                        R[t][pb] = jnp.where(rows8 == pr, u, R[t][pb] - jnp.where(rows8 > pr, l[pb], 0.0) * u)
                    else:
                        R[t][pb] = jnp.where(rows8 == pr, u, R[t][pb])
                    for b in range(pb + 1, nb):
                        R[t][b] = R[t][b] - l[b] * u
            R = [jnp.concatenate(x, axis=0) for x in R]
            for t in range(2):
                w_ref[r0:r0 + SB, wide[t] * NB:(wide[t] + 1) * NB] = R[t]
            if s < NB // SB - 1:
                X = jnp.concatenate(R, axis=1)
                xhi, xlo = split2(X)
                r1 = r0 + SB
                lh, ll = xhi[:, :NB], xlo[:, :NB]
                L = jnp.concatenate([lh, lh, ll], axis=0).T
                Rr = jnp.concatenate([xhi, xlo, xhi], axis=0)
                cuts = [(r1, NB)]
                for lo_, hi_ in cuts:
                    if lo_ < hi_:
                        upd = jnp.dot(L[lo_:hi_], Rr, preferred_element_type=jnp.float32)
                        for t in range(2):
                            sl = slice(wide[t] * NB, (wide[t] + 1) * NB)
                            w_ref[lo_:hi_, sl] = w_ref[lo_:hi_, sl] - upd[:, t * NB:(t + 1) * NB]
        lhi, llo = split2(w_ref[:, STEPS * NB:])
        shi, slo = split2(w_ref[:, NB:STEPS * NB])
        w_ref[:, NB:STEPS * NB] = jnp.dot(jnp.concatenate([lhi, lhi, llo], axis=1), jnp.concatenate([shi, slo, shi], axis=0), preferred_element_type=jnp.float32)
        tri = lax.broadcasted_iota(jnp.int32, (NB, NB), 0) <= lax.broadcasted_iota(jnp.int32, (NB, NB), 1)
        for t in range(STEPS):
            j = lax.rem(k + t, STEPS)
            jj = pl.multiple_of(j * NB, NB)
            keep = k + t < STEPS
            x = w_ref[:, t * NB:(t + 1) * NB]
            if t == 0:
                x = jnp.where(tri, x, 0.0)
                logs = logs + jnp.sum(jnp.log(jnp.sum(x * eye, axis=0, keepdims=True)), axis=1, keepdims=True)
            else:
                x = jnp.where(keep, x, 0.0)
            ub_ref[pl.ds(kk, NB), pl.ds(jj, NB)] = x.astype(jnp.bfloat16)
        linv_ref[k] = w_ref[:, STEPS * NB:]
        return logs

    logs = step(0, jnp.zeros((1, 1), jnp.float32))
    tops.wait()
    logs = lax.fori_loop(1, STEPS, step, logs)
    columns(STEPS - 1)
    logdet_ref[...] = logs * (2.0 / (STEPS * NB))

def chain(place, mine, other, top):
    return pl.pallas_call(
        chain_kernel,
        out_shape=(jax.ShapeDtypeStruct((STEPS * NB, STEPS * NB), jnp.bfloat16),
                   jax.ShapeDtypeStruct((STEPS, NB, NB), jnp.float32),
                   jax.ShapeDtypeStruct((STEPS * NB, LT * NB), jnp.bfloat16),
                   jax.ShapeDtypeStruct((1, 1), jnp.float32)),
        in_specs=[pl.BlockSpec(memory_space=pltpu.SMEM)] + [pl.BlockSpec(memory_space=pltpu.VMEM)] * 2 + [pl.BlockSpec(memory_space=pltpu.HBM)],
        out_specs=(pl.BlockSpec(memory_space=pltpu.VMEM),) * 4,
        scratch_shapes=[pltpu.VMEM((NB, (STEPS + 1) * NB), jnp.float32), pltpu.VMEM((2, HALF, NB, NB), jnp.float32),
                        pltpu.VMEM((STEPS, LT, NB, NB), jnp.float32), pltpu.SemaphoreType.DMA],
        compiler_params=pltpu.CompilerParams(vmem_limit_bytes=50 * 2**20),
        cost_estimate=pl.CostEstimate(flops=30_000_000_000, bytes_accessed=4 * 2**20, transcendentals=0),
        name="chain",
    )(place, mine, other, top)


def finish_kernel(place_ref, a_hbm, rp_ref, q_ref, ub_ref, linv_ref, pf_hbm, tr_hbm, a_ref, p_ref, b_ref, in_sem, p_sem, t_sem):
    row = place_ref[0]
    pairs = LT // 2
    loads = [pltpu.make_async_copy(a_hbm.at[:, pl.ds(2 * n, 2)], a_ref.at[n], in_sem.at[n]) for n in range(pairs)]
    for copy in loads:
        copy.start()
    ri = lax.broadcasted_iota(jnp.int32, (NB, NB), 0)
    ci = lax.broadcasted_iota(jnp.int32, (NB, NB), 1)
    scale = jnp.exp2(rp_ref[:, STEPS * LT * 8:STEPS * LT * 8 + 8] - SHIFT).reshape(NB, NB)
    stores = []
    later = None
    for k in range(STEPS):
        lhi, llo = split2(linv_ref[k])
        tiles = [rp_ref[:, (k * LT + l) * 8:(k * LT + l + 1) * 8].reshape(NB, NB) * scale for l in range(LT)]
        s = jnp.concatenate(tiles, axis=0)
        if k % 2 == 0:
            if k:
                both = jnp.dot(b_ref[:, :k * NB], ub_ref[:k * NB, k * NB:(k + 2) * NB], preferred_element_type=jnp.float32)
                s = s - both[:, :NB]
                later = both[:, NB:]
        else:
            s = s - jnp.dot(b_ref[:, (k - 1) * NB:k * NB], ub_ref[(k - 1) * NB:k * NB, k * NB:(k + 1) * NB],
                            preferred_element_type=jnp.float32)
            if k > 1:
                s = s - later
        shi, slo = split2(s)
        zero = jnp.zeros_like(llo)
        weights = jnp.concatenate([jnp.concatenate([lhi, lhi], axis=1), jnp.concatenate([llo, zero], axis=1)], axis=0)
        p = lax.dot_general(jnp.concatenate([shi, slo], axis=1), weights, (((1,), (1,)), ((), ())),
                            preferred_element_type=jnp.float32)
        p = p[:, :NB] + p[:, NB:]
        keep = jnp.where(row == k, ri - ci, row - k) >= 0
        first = jnp.where(keep, p[:NB], 0.0)
        p_ref[0, k] = first
        for l in range(1, LT):
            p_ref[l, k] = p[l * NB:(l + 1) * NB]
        b_ref[:NB, k * NB:(k + 1) * NB] = first.astype(jnp.bfloat16)
        b_ref[NB:, k * NB:(k + 1) * NB] = p[NB:].astype(jnp.bfloat16)
        store = pltpu.make_async_copy(p_ref.at[:, k], pf_hbm.at[:, k], p_sem.at[k])
        store.start()
        stores.append(store)
    for n in range(pairs):
        loads[n].wait()
        upd = jnp.dot(b_ref[...], q_ref[:, 2 * n * NB:2 * (n + 1) * NB], preferred_element_type=jnp.float32)
        for l in range(LT):
            for m in range(2):
                a_ref[n, l, m] = a_ref[n, l, m] - upd[l * NB:(l + 1) * NB, m * NB:(m + 1) * NB]
        store = pltpu.make_async_copy(a_ref.at[n], tr_hbm.at[:, pl.ds(2 * n, 2)], t_sem.at[n])
        store.start()
        stores.append(store)
    for store in stores:
        store.wait()


def finish(place, a, rp, q, ub, linv):
    vm = pl.BlockSpec(memory_space=pltpu.VMEM)
    hb = pl.BlockSpec(memory_space=pltpu.HBM)
    return pl.pallas_call(
        finish_kernel,
        out_shape=(jax.ShapeDtypeStruct((LT, STEPS, NB, NB), jnp.float32),
                   jax.ShapeDtypeStruct((LT, LT, NB, NB), jnp.float32)),
        in_specs=[pl.BlockSpec(memory_space=pltpu.SMEM), hb, vm, vm, vm, vm],
        out_specs=(hb, hb),
        scratch_shapes=[pltpu.VMEM((LT // 2, LT, 2, NB, NB), jnp.float32), pltpu.VMEM((LT, STEPS, NB, NB), jnp.float32),
                        pltpu.VMEM((LT * NB, STEPS * NB), jnp.bfloat16), pltpu.SemaphoreType.DMA((LT // 2,)),
                        pltpu.SemaphoreType.DMA((STEPS,)), pltpu.SemaphoreType.DMA((LT // 2,))],
        compiler_params=pltpu.CompilerParams(vmem_limit_bytes=44 * 2**20),
        cost_estimate=pl.CostEstimate(flops=4_000_000_000, bytes_accessed=14 * 2**20, transcendentals=0),
        name="finish",
    )(place, a, rp, q, ub, linv)


def spread_kernel(x_ref, o_ref):
    tiles = [x_ref[p, q] for p in range(STEPS // 2) for q in range(2 * p, STEPS)]
    for j in range(16):
        for n, tile in enumerate(tiles):
            o_ref[j, n] = tile


def spread_half(x):
    return pl.pallas_call(
        spread_kernel,
        out_shape=jax.ShapeDtypeStruct((16, HALF, 8, NB), jnp.float32),
        in_specs=[pl.BlockSpec(memory_space=pltpu.VMEM)],
        out_specs=pl.BlockSpec(memory_space=pltpu.VMEM),
        compiler_params=pltpu.CompilerParams(vmem_limit_bytes=4 * 2**20),
        name="spread",
    )(x)


def packed(x):
    top = jnp.maximum(jnp.max(jnp.abs(x)), 1e-30)
    power = jnp.floor(jnp.log2(top))
    body = (x * jnp.exp2(SHIFT - power)).astype(jnp.float16)
    return jnp.concatenate([body, jnp.full((16, NB), power, jnp.float16)], axis=0)


def shards(covariance):
    matrix = covariance[:, 0, :, 0]
    row = lax.axis_index("row")
    place = jnp.stack([row, lax.axis_index("col")]).astype(jnp.int32)
    across = lax.all_gather(matrix[0], "row", axis=0, tiled=False)
    first = matrix[:, 0].reshape(LT, 16, 8, NB).transpose(1, 0, 2, 3).reshape(16 * LT * 8, NB)
    slabs = lax.all_to_all(first, "col", 0, 0, tiled=True).reshape(16, LT, 8, NB)[:STEPS]
    sent = jnp.broadcast_to(slabs[None, :, 0], (8, STEPS, 8, NB))
    groups = [[2 * z + c for z in range(8)] for c in range(2)]
    lead = lax.all_to_all(sent, "row", 0, 0, tiled=True, axis_index_groups=groups)
    mine = lax.all_to_all(spread_half(lead), "col", 0, 0, tiled=True)
    other = lax.ppermute(mine, "row", [(i, i ^ 1) for i in range(16)])
    half = packed(slabs.reshape(STEPS * LT * 8, NB))
    half, mine = lax.optimization_barrier((jnp.broadcast_to(half[None], (16,) + half.shape), mine))
    down = lax.all_to_all(half, "col", 0, 0, tiled=True)
    ub, linv, q, logdet = chain(place, mine, other, across)
    down, q = lax.optimization_barrier((down, q))
    panel, trailing = finish(place, matrix, down.astype(jnp.float32), q, ub, linv)
    return panel[:, None], trailing[:, None, :, None], logdet[0, 0]


def solution(mesh):
    in_specs = (P(None, "row", None, "col", None, None),)
    out_specs = (P(None, "row", None, None, None), P(None, "row", None, "col", None, None), P())
    return jax.shard_map(shards, mesh=mesh, in_specs=in_specs, out_specs=out_specs, check_vma=False)
```

```python
import jax
import jax.numpy as jnp
from jax import lax
from jax.experimental import pallas as pl
from jax.experimental.pallas import tpu as pltpu
from jax.sharding import PartitionSpec as P

STEPS = 6
NB = 128
LT = 8
SB = 32
HALF = 12
SHIFT = 13.0


def split2(x):
    hi = x.astype(jnp.bfloat16)
    lo = (x - hi.astype(jnp.float32)).astype(jnp.bfloat16)
    return hi, lo

def chain_kernel(place_ref, mine_ref, other_ref, top_hbm, ub_ref, linv_ref, q_ref, logdet_ref, w_ref, d_ref, top_ref, sem):
    tops = pltpu.make_async_copy(top_hbm.at[pl.ds(0, STEPS)], top_ref, sem)
    tops.start()
    col = place_ref[1]
    core = lax.rem(place_ref[0], 2)
    for n in range(HALF):
        d_ref[core, n] = mine_ref[:, n].reshape(NB, NB)
        d_ref[1 - core, n] = other_ref[:, n].reshape(NB, NB)
    ub_ref[...] = jnp.zeros_like(ub_ref)
    q_ref[...] = jnp.zeros_like(q_ref)
    eye = (lax.broadcasted_iota(jnp.int32, (NB, NB), 0) == lax.broadcasted_iota(jnp.int32, (NB, NB), 1)).astype(jnp.float32)
    rows8 = lax.broadcasted_iota(jnp.int32, (8, NB), 0)
    ri = lax.broadcasted_iota(jnp.int32, (NB, NB), 0)
    ci = lax.broadcasted_iota(jnp.int32, (NB, NB), 1)

    def columns(k):
        kk = pl.multiple_of(k * NB, NB)
        lhi, llo = split2(linv_ref[k])
        x = jnp.concatenate([top_ref[k, m] for m in range(LT)], axis=1)
        x = x - lax.dot_general(ub_ref[:, pl.ds(kk, NB)], q_ref[...], (((0,), (0,)), ((), ())),
                                preferred_element_type=jnp.float32)
        xhi, xlo = split2(x)
        q = jnp.dot(jnp.concatenate([lhi, lhi, llo], axis=1), jnp.concatenate([xhi, xlo, xhi], axis=0),
                    preferred_element_type=jnp.float32)
        keep = jnp.where(col == k, ci - ri, col - k) >= 0
        q_ref[pl.ds(kk, NB), :NB] = jnp.where(keep, q[:, :NB], 0.0).astype(jnp.bfloat16)
        q_ref[pl.ds(kk, NB), NB:] = q[:, NB:].astype(jnp.bfloat16)

    def step(k, logs):
        kk = pl.multiple_of(k * NB, NB)
        left = ub_ref[:, pl.ds(kk, NB)]
        for t in range(STEPS):
            j = lax.rem(k + t, STEPS)
            jj = pl.multiple_of(j * NB, NB)
            low, high = jnp.minimum(k, j), jnp.maximum(k, j)
            pair = low // 2
            place = pair * STEPS - pair * (pair - 1) + high - 2 * pair
            upd = lax.dot_general(left, ub_ref[:, pl.ds(jj, NB)], (((0,), (0,)), ((), ())), preferred_element_type=jnp.float32)
            w_ref[:, t * NB:(t + 1) * NB] = d_ref[lax.rem(low, 2), place] - upd
        w_ref[:, STEPS * NB:] = eye
        if not isinstance(k, int):
            columns(k - 1)
        wide = (0, STEPS)
        for s in range(NB // SB):
            r0 = s * SB
            nb = SB // 8
            R = [[w_ref[r0 + 8 * b:r0 + 8 * b + 8, t * NB:(t + 1) * NB] for b in range(nb)] for t in wide]
            cols = [{b: jnp.broadcast_to(R[0][b][:, r0 + q:r0 + q + 1], (8, NB)) for b in range(q // 8, nb)} for q in range(SB)]
            for p in range(SB):
                pb, pr = p // 8, p % 8
                inv = lax.rsqrt(jnp.broadcast_to(cols[p][pb][pr:pr + 1, :], (8, NB)))
                l = {b: cols[p][b] * inv for b in range(pb, nb)}
                for q in range(p + 1, SB):
                    m = jnp.broadcast_to(l[q // 8][q % 8:q % 8 + 1, :], (8, NB))
                    for b in range(q // 8, nb):
                        cols[q][b] = cols[q][b] - l[b] * m
                for t in range(2):
                    u = jnp.broadcast_to(R[t][pb][pr:pr + 1, :], (8, NB)) * inv
                    if pr < 7:
                        R[t][pb] = jnp.where(rows8 == pr, u, R[t][pb] - jnp.where(rows8 > pr, l[pb], 0.0) * u)
                    else:
                        R[t][pb] = jnp.where(rows8 == pr, u, R[t][pb])
                    for b in range(pb + 1, nb):
                        R[t][b] = R[t][b] - l[b] * u
            R = [jnp.concatenate(x, axis=0) for x in R]
            for t in range(2):
                w_ref[r0:r0 + SB, wide[t] * NB:(wide[t] + 1) * NB] = R[t]
            if s < NB // SB - 1:
                X = jnp.concatenate(R, axis=1)
                xhi, xlo = split2(X)
                r1 = r0 + SB
                lh, ll = xhi[:, :NB], xlo[:, :NB]
                L = jnp.concatenate([lh, lh, ll], axis=0).T
                Rr = jnp.concatenate([xhi, xlo, xhi], axis=0)
                cuts = [(r1, NB)]
                for lo_, hi_ in cuts:
                    if lo_ < hi_:
                        upd = jnp.dot(L[lo_:hi_], Rr, preferred_element_type=jnp.float32)
                        for t in range(2):
                            sl = slice(wide[t] * NB, (wide[t] + 1) * NB)
                            w_ref[lo_:hi_, sl] = w_ref[lo_:hi_, sl] - upd[:, t * NB:(t + 1) * NB]
        lhi, llo = split2(w_ref[:, STEPS * NB:])
        shi, slo = split2(w_ref[:, NB:STEPS * NB])
        w_ref[:, NB:STEPS * NB] = jnp.dot(jnp.concatenate([lhi, lhi, llo], axis=1), jnp.concatenate([shi, slo, shi], axis=0), preferred_element_type=jnp.float32)
        tri = lax.broadcasted_iota(jnp.int32, (NB, NB), 0) <= lax.broadcasted_iota(jnp.int32, (NB, NB), 1)
        for t in range(STEPS):
            j = lax.rem(k + t, STEPS)
            jj = pl.multiple_of(j * NB, NB)
            keep = k + t < STEPS
            x = w_ref[:, t * NB:(t + 1) * NB]
            if t == 0:
                x = jnp.where(tri, x, 0.0)
                logs = logs + jnp.sum(jnp.log(jnp.sum(x * eye, axis=0, keepdims=True)), axis=1, keepdims=True)
            else:
                x = jnp.where(keep, x, 0.0)
            ub_ref[pl.ds(kk, NB), pl.ds(jj, NB)] = x.astype(jnp.bfloat16)
        linv_ref[k] = w_ref[:, STEPS * NB:]
        return logs

    logs = step(0, jnp.zeros((1, 1), jnp.float32))
    tops.wait()
    logs = lax.fori_loop(1, STEPS, step, logs)
    columns(STEPS - 1)
    logdet_ref[...] = logs * (2.0 / (STEPS * NB))

def chain(place, mine, other, top):
    return pl.pallas_call(
        chain_kernel,
        out_shape=(jax.ShapeDtypeStruct((STEPS * NB, STEPS * NB), jnp.bfloat16),
                   jax.ShapeDtypeStruct((STEPS, NB, NB), jnp.float32),
                   jax.ShapeDtypeStruct((STEPS * NB, LT * NB), jnp.bfloat16),
                   jax.ShapeDtypeStruct((1, 1), jnp.float32)),
        in_specs=[pl.BlockSpec(memory_space=pltpu.SMEM)] + [pl.BlockSpec(memory_space=pltpu.VMEM)] * 2 + [pl.BlockSpec(memory_space=pltpu.HBM)],
        out_specs=(pl.BlockSpec(memory_space=pltpu.VMEM),) * 4,
        scratch_shapes=[pltpu.VMEM((NB, (STEPS + 1) * NB), jnp.float32), pltpu.VMEM((2, HALF, NB, NB), jnp.float32),
                        pltpu.VMEM((STEPS, LT, NB, NB), jnp.float32), pltpu.SemaphoreType.DMA],
        compiler_params=pltpu.CompilerParams(vmem_limit_bytes=50 * 2**20),
        cost_estimate=pl.CostEstimate(flops=30_000_000_000, bytes_accessed=4 * 2**20, transcendentals=0),
        name="chain",
    )(place, mine, other, top)


def finish_kernel(place_ref, a_hbm, rp_ref, q_ref, ub_ref, linv_ref, pf_hbm, tr_hbm, a_ref, p_ref, b_ref, in_sem, p_sem, t_sem):
    row = place_ref[0]
    pairs = LT // 2
    loads = [pltpu.make_async_copy(a_hbm.at[:, pl.ds(2 * n, 2)], a_ref.at[n], in_sem.at[n]) for n in range(pairs)]
    for copy in loads:
        copy.start()
    ri = lax.broadcasted_iota(jnp.int32, (NB, NB), 0)
    ci = lax.broadcasted_iota(jnp.int32, (NB, NB), 1)
    scale = jnp.exp2(rp_ref[:, STEPS * LT * 8:STEPS * LT * 8 + 8] - SHIFT).reshape(NB, NB)
    stores = []
    later = None
    for k in range(STEPS):
        lhi, llo = split2(linv_ref[k])
        tiles = [rp_ref[:, (k * LT + l) * 8:(k * LT + l + 1) * 8].reshape(NB, NB) * scale for l in range(LT)]
        s = jnp.concatenate(tiles, axis=0)
        if k % 2 == 0:
            if k:
                both = jnp.dot(b_ref[:, :k * NB], ub_ref[:k * NB, k * NB:(k + 2) * NB], preferred_element_type=jnp.float32)
                s = s - both[:, :NB]
                later = both[:, NB:]
        else:
            s = s - jnp.dot(b_ref[:, (k - 1) * NB:k * NB], ub_ref[(k - 1) * NB:k * NB, k * NB:(k + 1) * NB],
                            preferred_element_type=jnp.float32)
            if k > 1:
                s = s - later
        shi, slo = split2(s)
        zero = jnp.zeros_like(llo)
        weights = jnp.concatenate([jnp.concatenate([lhi, lhi], axis=1), jnp.concatenate([llo, zero], axis=1)], axis=0)
        p = lax.dot_general(jnp.concatenate([shi, slo], axis=1), weights, (((1,), (1,)), ((), ())),
                            preferred_element_type=jnp.float32)
        p = p[:, :NB] + p[:, NB:]
        keep = jnp.where(row == k, ri - ci, row - k) >= 0
        first = jnp.where(keep, p[:NB], 0.0)
        p_ref[0, k] = first
        for l in range(1, LT):
            p_ref[l, k] = p[l * NB:(l + 1) * NB]
        b_ref[:NB, k * NB:(k + 1) * NB] = first.astype(jnp.bfloat16)
        b_ref[NB:, k * NB:(k + 1) * NB] = p[NB:].astype(jnp.bfloat16)
        store = pltpu.make_async_copy(p_ref.at[:, k], pf_hbm.at[:, k], p_sem.at[k])
        store.start()
        stores.append(store)
        if k % 2 == 0:
            continue
        for n in range(pairs):
            if k == 1:
                loads[n].wait()
            upd = jnp.dot(b_ref[:, (k - 1) * NB:(k + 1) * NB], q_ref[(k - 1) * NB:(k + 1) * NB, 2 * n * NB:2 * (n + 1) * NB],
                          preferred_element_type=jnp.float32)
            for l in range(LT):
                for m in range(2):
                    a_ref[n, l, m] = a_ref[n, l, m] - upd[l * NB:(l + 1) * NB, m * NB:(m + 1) * NB]
            if k == STEPS - 1:
                store = pltpu.make_async_copy(a_ref.at[n], tr_hbm.at[:, pl.ds(2 * n, 2)], t_sem.at[n])
                store.start()
                stores.append(store)
    for store in stores:
        store.wait()


def finish(place, a, rp, q, ub, linv):
    vm = pl.BlockSpec(memory_space=pltpu.VMEM)
    hb = pl.BlockSpec(memory_space=pltpu.HBM)
    return pl.pallas_call(
        finish_kernel,
        out_shape=(jax.ShapeDtypeStruct((LT, STEPS, NB, NB), jnp.float32),
                   jax.ShapeDtypeStruct((LT, LT, NB, NB), jnp.float32)),
        in_specs=[pl.BlockSpec(memory_space=pltpu.SMEM), hb, vm, vm, vm, vm],
        out_specs=(hb, hb),
        scratch_shapes=[pltpu.VMEM((LT // 2, LT, 2, NB, NB), jnp.float32), pltpu.VMEM((LT, STEPS, NB, NB), jnp.float32),
                        pltpu.VMEM((LT * NB, STEPS * NB), jnp.bfloat16), pltpu.SemaphoreType.DMA((LT // 2,)),
                        pltpu.SemaphoreType.DMA((STEPS,)), pltpu.SemaphoreType.DMA((LT // 2,))],
        compiler_params=pltpu.CompilerParams(vmem_limit_bytes=44 * 2**20),
        cost_estimate=pl.CostEstimate(flops=4_000_000_000, bytes_accessed=14 * 2**20, transcendentals=0),
        name="finish",
    )(place, a, rp, q, ub, linv)


def cut_kernel(a_hbm, top_hbm, first_ref, top_sem, sem):
    top = pltpu.make_async_copy(a_hbm.at[0], top_hbm, top_sem)
    top.start()
    cuts = [pltpu.make_async_copy(a_hbm.at[l, 0], first_ref.at[:, l], sem.at[l]) for l in range(LT)]
    for copy in cuts:
        copy.start()
    for copy in cuts + [top]:
        copy.wait()


def cut(a):
    return pl.pallas_call(
        cut_kernel,
        out_shape=(jax.ShapeDtypeStruct((LT, 16, 8, NB), jnp.float32), jax.ShapeDtypeStruct((16, LT, 8, NB), jnp.float32)),
        in_specs=[pl.BlockSpec(memory_space=pltpu.HBM)],
        out_specs=(pl.BlockSpec(memory_space=pltpu.HBM), pl.BlockSpec(memory_space=pltpu.VMEM)),
        scratch_shapes=[pltpu.SemaphoreType.DMA, pltpu.SemaphoreType.DMA((LT,))],
        compiler_params=pltpu.CompilerParams(vmem_limit_bytes=58 * 2**20),
        name="cut",
    )(a)


def spread_kernel(x_ref, o_ref):
    tiles = [x_ref[p, q] for p in range(STEPS // 2) for q in range(2 * p, STEPS)]
    for j in range(16):
        for n, tile in enumerate(tiles):
            o_ref[j, n] = tile


def spread_half(x):
    return pl.pallas_call(
        spread_kernel,
        out_shape=jax.ShapeDtypeStruct((16, HALF, 8, NB), jnp.float32),
        in_specs=[pl.BlockSpec(memory_space=pltpu.VMEM)],
        out_specs=pl.BlockSpec(memory_space=pltpu.VMEM),
        compiler_params=pltpu.CompilerParams(vmem_limit_bytes=4 * 2**20),
        name="spread",
    )(x)


def packed(x):
    top = jnp.maximum(jnp.max(jnp.abs(x)), 1e-30)
    power = jnp.floor(jnp.log2(top))
    body = (x * jnp.exp2(SHIFT - power)).astype(jnp.float16)
    return jnp.concatenate([body, jnp.full((16, NB), power, jnp.float16)], axis=0)


def shards(covariance):
    matrix = covariance[:, 0, :, 0]
    row = lax.axis_index("row")
    place = jnp.stack([row, lax.axis_index("col")]).astype(jnp.int32)
    top, first = cut(matrix.reshape(LT, LT, 16, 8, NB))
    across = lax.all_gather(top.reshape(LT, NB, NB), "row", axis=0, tiled=False)
    slabs = lax.all_to_all(first.reshape(16 * LT * 8, NB), "col", 0, 0, tiled=True).reshape(16, LT, 8, NB)[:STEPS]
    sent = jnp.broadcast_to(slabs[None, :, 0], (8, STEPS, 8, NB))
    groups = [[2 * z + c for z in range(8)] for c in range(2)]
    lead = lax.all_to_all(sent, "row", 0, 0, tiled=True, axis_index_groups=groups)
    mine = lax.all_to_all(spread_half(lead), "col", 0, 0, tiled=True)
    other = lax.ppermute(mine, "row", [(i, i ^ 1) for i in range(16)])
    half = packed(slabs.reshape(STEPS * LT * 8, NB))
    half, mine = lax.optimization_barrier((jnp.broadcast_to(half[None], (16,) + half.shape), mine))
    down = lax.all_to_all(half, "col", 0, 0, tiled=True)
    ub, linv, q, logdet = chain(place, mine, other, across)
    down, q = lax.optimization_barrier((down, q))
    panel, trailing = finish(place, matrix, down.astype(jnp.float32), q, ub, linv)
    return panel[:, None], trailing[:, None, :, None], logdet[0, 0]


def solution(mesh):
    in_specs = (P(None, "row", None, "col", None, None),)
    out_specs = (P(None, "row", None, None, None), P(None, "row", None, "col", None, None), P())
    return jax.shard_map(shards, mesh=mesh, in_specs=in_specs, out_specs=out_specs, check_vma=False)
```

```python
import jax
import jax.numpy as jnp
from jax import lax
from jax.experimental import pallas as pl
from jax.experimental.pallas import tpu as pltpu
from jax.sharding import PartitionSpec as P

STEPS = 6
NB = 128
LT = 8
SB = 32
HALF = 12
SHIFT = 13.0


def split2(x):
    hi = x.astype(jnp.bfloat16)
    lo = (x - hi.astype(jnp.float32)).astype(jnp.bfloat16)
    return hi, lo

def chain_kernel(place_ref, mine_ref, other_ref, top_hbm, ub_ref, linv_ref, q_ref, logdet_ref, w_ref, d_ref, top_ref, sem):
    tops = pltpu.make_async_copy(top_hbm.at[pl.ds(0, STEPS)], top_ref, sem)
    tops.start()
    col = place_ref[1]
    core = lax.rem(place_ref[0], 2)
    for n in range(HALF):
        d_ref[core, n] = mine_ref[:, n].reshape(NB, NB)
        d_ref[1 - core, n] = other_ref[:, n].reshape(NB, NB)
    ub_ref[...] = jnp.zeros_like(ub_ref)
    q_ref[...] = jnp.zeros_like(q_ref)
    eye = (lax.broadcasted_iota(jnp.int32, (NB, NB), 0) == lax.broadcasted_iota(jnp.int32, (NB, NB), 1)).astype(jnp.float32)
    rows8 = lax.broadcasted_iota(jnp.int32, (8, NB), 0)
    ri = lax.broadcasted_iota(jnp.int32, (NB, NB), 0)
    ci = lax.broadcasted_iota(jnp.int32, (NB, NB), 1)

    def columns(k):
        kk = pl.multiple_of(k * NB, NB)
        lhi, llo = split2(linv_ref[k])
        x = jnp.concatenate([top_ref[k, m] for m in range(LT)], axis=1)
        x = x - lax.dot_general(ub_ref[:, pl.ds(kk, NB)], q_ref[...], (((0,), (0,)), ((), ())),
                                preferred_element_type=jnp.float32)
        xhi, xlo = split2(x)
        q = jnp.dot(jnp.concatenate([lhi, lhi, llo], axis=1), jnp.concatenate([xhi, xlo, xhi], axis=0),
                    preferred_element_type=jnp.float32)
        keep = jnp.where(col == k, ci - ri, col - k) >= 0
        q_ref[pl.ds(kk, NB), :NB] = jnp.where(keep, q[:, :NB], 0.0).astype(jnp.bfloat16)
        q_ref[pl.ds(kk, NB), NB:] = q[:, NB:].astype(jnp.bfloat16)

    def step(k, logs):
        kk = pl.multiple_of(k * NB, NB)
        left = ub_ref[:, pl.ds(kk, NB)]
        for t in range(STEPS):
            j = lax.rem(k + t, STEPS)
            jj = pl.multiple_of(j * NB, NB)
            low, high = jnp.minimum(k, j), jnp.maximum(k, j)
            pair = low // 2
            place = pair * STEPS - pair * (pair - 1) + high - 2 * pair
            upd = lax.dot_general(left, ub_ref[:, pl.ds(jj, NB)], (((0,), (0,)), ((), ())), preferred_element_type=jnp.float32)
            w_ref[:, t * NB:(t + 1) * NB] = d_ref[lax.rem(low, 2), place] - upd
        w_ref[:, STEPS * NB:] = eye
        if not isinstance(k, int):
            columns(k - 1)
        wide = (0, STEPS)
        for s in range(NB // SB):
            r0 = s * SB
            nb = SB // 8
            R = [[w_ref[r0 + 8 * b:r0 + 8 * b + 8, t * NB:(t + 1) * NB] for b in range(nb)] for t in wide]
            cols = [{b: jnp.broadcast_to(R[0][b][:, r0 + q:r0 + q + 1], (8, NB)) for b in range(q // 8, nb)} for q in range(SB)]
            for p in range(SB):
                pb, pr = p // 8, p % 8
                inv = lax.rsqrt(jnp.broadcast_to(cols[p][pb][pr:pr + 1, :], (8, NB)))
                l = {b: cols[p][b] * inv for b in range(pb, nb)}
                for q in range(p + 1, SB):
                    m = jnp.broadcast_to(l[q // 8][q % 8:q % 8 + 1, :], (8, NB))
                    for b in range(q // 8, nb):
                        cols[q][b] = cols[q][b] - l[b] * m
                for t in range(2):
                    u = jnp.broadcast_to(R[t][pb][pr:pr + 1, :], (8, NB)) * inv
                    if pr < 7:
                        R[t][pb] = jnp.where(rows8 == pr, u, R[t][pb] - jnp.where(rows8 > pr, l[pb], 0.0) * u)
                    else:
                        R[t][pb] = jnp.where(rows8 == pr, u, R[t][pb])
                    for b in range(pb + 1, nb):
                        R[t][b] = R[t][b] - l[b] * u
            R = [jnp.concatenate(x, axis=0) for x in R]
            for t in range(2):
                w_ref[r0:r0 + SB, wide[t] * NB:(wide[t] + 1) * NB] = R[t]
            if s < NB // SB - 1:
                X = jnp.concatenate(R, axis=1)
                xhi, xlo = split2(X)
                r1 = r0 + SB
                lh, ll = xhi[:, :NB], xlo[:, :NB]
                L = jnp.concatenate([lh, lh, ll], axis=0).T
                Rr = jnp.concatenate([xhi, xlo, xhi], axis=0)
                cuts = [(r1, NB)]
                for lo_, hi_ in cuts:
                    if lo_ < hi_:
                        upd = jnp.dot(L[lo_:hi_], Rr, preferred_element_type=jnp.float32)
                        for t in range(2):
                            sl = slice(wide[t] * NB, (wide[t] + 1) * NB)
                            w_ref[lo_:hi_, sl] = w_ref[lo_:hi_, sl] - upd[:, t * NB:(t + 1) * NB]
        lhi, llo = split2(w_ref[:, STEPS * NB:])
        shi, slo = split2(w_ref[:, NB:STEPS * NB])
        w_ref[:, NB:STEPS * NB] = jnp.dot(jnp.concatenate([lhi, lhi, llo], axis=1), jnp.concatenate([shi, slo, shi], axis=0), preferred_element_type=jnp.float32)
        tri = lax.broadcasted_iota(jnp.int32, (NB, NB), 0) <= lax.broadcasted_iota(jnp.int32, (NB, NB), 1)
        for t in range(STEPS):
            j = lax.rem(k + t, STEPS)
            jj = pl.multiple_of(j * NB, NB)
            keep = k + t < STEPS
            x = w_ref[:, t * NB:(t + 1) * NB]
            if t == 0:
                x = jnp.where(tri, x, 0.0)
                logs = logs + jnp.sum(jnp.log(jnp.sum(x * eye, axis=0, keepdims=True)), axis=1, keepdims=True)
            else:
                x = jnp.where(keep, x, 0.0)
            ub_ref[pl.ds(kk, NB), pl.ds(jj, NB)] = x.astype(jnp.bfloat16)
        linv_ref[k] = w_ref[:, STEPS * NB:]
        return logs

    logs = step(0, jnp.zeros((1, 1), jnp.float32))
    tops.wait()
    logs = lax.fori_loop(1, STEPS, step, logs)
    columns(STEPS - 1)
    logdet_ref[...] = logs * (2.0 / (STEPS * NB))

def chain(place, mine, other, top):
    return pl.pallas_call(
        chain_kernel,
        out_shape=(jax.ShapeDtypeStruct((STEPS * NB, STEPS * NB), jnp.bfloat16),
                   jax.ShapeDtypeStruct((STEPS, NB, NB), jnp.float32),
                   jax.ShapeDtypeStruct((STEPS * NB, LT * NB), jnp.bfloat16),
                   jax.ShapeDtypeStruct((1, 1), jnp.float32)),
        in_specs=[pl.BlockSpec(memory_space=pltpu.SMEM)] + [pl.BlockSpec(memory_space=pltpu.VMEM)] * 2 + [pl.BlockSpec(memory_space=pltpu.HBM)],
        out_specs=(pl.BlockSpec(memory_space=pltpu.VMEM),) * 4,
        scratch_shapes=[pltpu.VMEM((NB, (STEPS + 1) * NB), jnp.float32), pltpu.VMEM((2, HALF, NB, NB), jnp.float32),
                        pltpu.VMEM((STEPS, LT, NB, NB), jnp.float32), pltpu.SemaphoreType.DMA],
        compiler_params=pltpu.CompilerParams(vmem_limit_bytes=50 * 2**20),
        cost_estimate=pl.CostEstimate(flops=30_000_000_000, bytes_accessed=4 * 2**20, transcendentals=0),
        name="chain",
    )(place, mine, other, top)


def finish_kernel(place_ref, a_hbm, rp_ref, q_ref, ub_ref, linv_ref, pf_hbm, tr_hbm, a_ref, p_ref, b_ref, in_sem, p_sem, t_sem):
    row = place_ref[0]
    pairs = LT // 2
    loads = [pltpu.make_async_copy(a_hbm.at[:, pl.ds(2 * n, 2)], a_ref.at[n], in_sem.at[n]) for n in range(pairs)]
    for copy in loads:
        copy.start()
    ri = lax.broadcasted_iota(jnp.int32, (NB, NB), 0)
    ci = lax.broadcasted_iota(jnp.int32, (NB, NB), 1)
    scale = jnp.exp2(rp_ref[:, STEPS * LT * 8:STEPS * LT * 8 + 8] - SHIFT).reshape(NB, NB)
    stores = []
    later = None
    for k in range(STEPS):
        lhi, llo = split2(linv_ref[k])
        tiles = [rp_ref[:, (k * LT + l) * 8:(k * LT + l + 1) * 8].reshape(NB, NB) * scale for l in range(LT)]
        s = jnp.concatenate(tiles, axis=0)
        if k % 2 == 0:
            if k:
                both = jnp.dot(b_ref[:, :k * NB], ub_ref[:k * NB, k * NB:(k + 2) * NB], preferred_element_type=jnp.float32)
                s = s - both[:, :NB]
                later = both[:, NB:]
        else:
            s = s - jnp.dot(b_ref[:, (k - 1) * NB:k * NB], ub_ref[(k - 1) * NB:k * NB, k * NB:(k + 1) * NB],
                            preferred_element_type=jnp.float32)
            if k > 1:
                s = s - later
        shi, slo = split2(s)
        zero = jnp.zeros_like(llo)
        weights = jnp.concatenate([jnp.concatenate([lhi, lhi], axis=1), jnp.concatenate([llo, zero], axis=1)], axis=0)
        p = lax.dot_general(jnp.concatenate([shi, slo], axis=1), weights, (((1,), (1,)), ((), ())),
                            preferred_element_type=jnp.float32)
        p = p[:, :NB] + p[:, NB:]
        keep = jnp.where(row == k, ri - ci, row - k) >= 0
        first = jnp.where(keep, p[:NB], 0.0)
        p_ref[0, k] = first
        for l in range(1, LT):
            p_ref[l, k] = p[l * NB:(l + 1) * NB]
        b_ref[:NB, k * NB:(k + 1) * NB] = first.astype(jnp.bfloat16)
        b_ref[NB:, k * NB:(k + 1) * NB] = p[NB:].astype(jnp.bfloat16)
        store = pltpu.make_async_copy(p_ref.at[:, k], pf_hbm.at[:, k], p_sem.at[k])
        store.start()
        stores.append(store)
        if k % 2 == 0:
            continue
        for n in range(pairs):
            if k == 1:
                loads[n].wait()
            upd = jnp.dot(b_ref[:, (k - 1) * NB:(k + 1) * NB], q_ref[(k - 1) * NB:(k + 1) * NB, 2 * n * NB:2 * (n + 1) * NB],
                          preferred_element_type=jnp.float32)
            for l in range(LT):
                for m in range(2):
                    a_ref[n, l, m] = a_ref[n, l, m] - upd[l * NB:(l + 1) * NB, m * NB:(m + 1) * NB]
            if k == STEPS - 1:
                store = pltpu.make_async_copy(a_ref.at[n], tr_hbm.at[:, pl.ds(2 * n, 2)], t_sem.at[n])
                store.start()
                stores.append(store)
    for store in stores:
        store.wait()


def finish(place, a, rp, q, ub, linv):
    vm = pl.BlockSpec(memory_space=pltpu.VMEM)
    hb = pl.BlockSpec(memory_space=pltpu.HBM)
    return pl.pallas_call(
        finish_kernel,
        out_shape=(jax.ShapeDtypeStruct((LT, STEPS, NB, NB), jnp.float32),
                   jax.ShapeDtypeStruct((LT, LT, NB, NB), jnp.float32)),
        in_specs=[pl.BlockSpec(memory_space=pltpu.SMEM), hb, vm, vm, vm, vm],
        out_specs=(hb, hb),
        scratch_shapes=[pltpu.VMEM((LT // 2, LT, 2, NB, NB), jnp.float32), pltpu.VMEM((LT, STEPS, NB, NB), jnp.float32),
                        pltpu.VMEM((LT * NB, STEPS * NB), jnp.bfloat16), pltpu.SemaphoreType.DMA((LT // 2,)),
                        pltpu.SemaphoreType.DMA((STEPS,)), pltpu.SemaphoreType.DMA((LT // 2,))],
        compiler_params=pltpu.CompilerParams(vmem_limit_bytes=44 * 2**20),
        cost_estimate=pl.CostEstimate(flops=4_000_000_000, bytes_accessed=14 * 2**20, transcendentals=0),
        name="finish",
    )(place, a, rp, q, ub, linv)


def spread_kernel(x_ref, o_ref):
    tiles = [x_ref[p, q] for p in range(STEPS // 2) for q in range(2 * p, STEPS)]
    for j in range(16):
        for n, tile in enumerate(tiles):
            o_ref[j, n] = tile


def spread_half(x):
    return pl.pallas_call(
        spread_kernel,
        out_shape=jax.ShapeDtypeStruct((16, HALF, 8, NB), jnp.float32),
        in_specs=[pl.BlockSpec(memory_space=pltpu.VMEM)],
        out_specs=pl.BlockSpec(memory_space=pltpu.VMEM),
        compiler_params=pltpu.CompilerParams(vmem_limit_bytes=4 * 2**20),
        name="spread",
    )(x)


def packed(x):
    top = jnp.maximum(jnp.max(jnp.abs(x)), 1e-30)
    power = jnp.floor(jnp.log2(top))
    body = (x * jnp.exp2(SHIFT - power)).astype(jnp.float16)
    return jnp.concatenate([body, jnp.full((16, NB), power, jnp.float16)], axis=0)


def shards(covariance):
    matrix = covariance[:, 0, :, 0]
    row = lax.axis_index("row")
    place = jnp.stack([row, lax.axis_index("col")]).astype(jnp.int32)
    across = lax.all_gather(matrix[0], "row", axis=0, tiled=False)
    first = matrix[:, 0].reshape(LT, 16, 8, NB).transpose(1, 0, 2, 3).reshape(16 * LT * 8, NB)
    slabs = lax.all_to_all(first, "col", 0, 0, tiled=True).reshape(16, LT, 8, NB)[:STEPS]
    sent = jnp.broadcast_to(slabs[None, :, 0], (8, STEPS, 8, NB))
    groups = [[2 * z + c for z in range(8)] for c in range(2)]
    lead = lax.all_to_all(sent, "row", 0, 0, tiled=True, axis_index_groups=groups)
    mine = lax.all_to_all(spread_half(lead), "col", 0, 0, tiled=True)
    other = lax.ppermute(mine, "row", [(i, i ^ 1) for i in range(16)])
    half = packed(slabs.reshape(STEPS * LT * 8, NB))
    half, mine = lax.optimization_barrier((jnp.broadcast_to(half[None], (16,) + half.shape), mine))
    down = lax.all_to_all(half, "col", 0, 0, tiled=True)
    ub, linv, q, logdet = chain(place, mine, other, across)
    down, q = lax.optimization_barrier((down, q))
    panel, trailing = finish(place, matrix, down.astype(jnp.float32), q, ub, linv)
    return panel[:, None], trailing[:, None, :, None], logdet[0, 0]


def solution(mesh):
    in_specs = (P(None, "row", None, "col", None, None),)
    out_specs = (P(None, "row", None, None, None), P(None, "row", None, "col", None, None), P())
    return jax.shard_map(shards, mesh=mesh, in_specs=in_specs, out_specs=out_specs, check_vma=False)
```

```python
import jax
import jax.numpy as jnp
from jax import lax
from jax.experimental import pallas as pl
from jax.experimental.pallas import tpu as pltpu
from jax.sharding import PartitionSpec as P

STEPS = 6
NB = 128
LT = 8
SB = 32
HALF = 12
SHIFT = 13.0


def split2(x):
    hi = x.astype(jnp.bfloat16)
    lo = (x - hi.astype(jnp.float32)).astype(jnp.bfloat16)
    return hi, lo

def chain_kernel(place_ref, mine_ref, other_ref, top_hbm, ub_ref, linv_ref, q_ref, logdet_ref, w_ref, d_ref, top_ref, sem):
    tops = pltpu.make_async_copy(top_hbm.at[pl.ds(0, STEPS)], top_ref, sem)
    tops.start()
    col = place_ref[1]
    core = lax.rem(place_ref[0], 2)
    for n in range(HALF):
        d_ref[core, n] = mine_ref[:, n].reshape(NB, NB)
        d_ref[1 - core, n] = other_ref[:, n].reshape(NB, NB)
    ub_ref[...] = jnp.zeros_like(ub_ref)
    q_ref[...] = jnp.zeros_like(q_ref)
    eye = (lax.broadcasted_iota(jnp.int32, (NB, NB), 0) == lax.broadcasted_iota(jnp.int32, (NB, NB), 1)).astype(jnp.float32)
    rows8 = lax.broadcasted_iota(jnp.int32, (8, NB), 0)
    ri = lax.broadcasted_iota(jnp.int32, (NB, NB), 0)
    ci = lax.broadcasted_iota(jnp.int32, (NB, NB), 1)

    def columns(k):
        kk = pl.multiple_of(k * NB, NB)
        lhi, llo = split2(linv_ref[k])
        x = jnp.concatenate([top_ref[k, m] for m in range(LT)], axis=1)
        x = x - lax.dot_general(ub_ref[:, pl.ds(kk, NB)], q_ref[...], (((0,), (0,)), ((), ())),
                                preferred_element_type=jnp.float32)
        xhi, xlo = split2(x)
        q = jnp.dot(jnp.concatenate([lhi, lhi, llo], axis=1), jnp.concatenate([xhi, xlo, xhi], axis=0),
                    preferred_element_type=jnp.float32)
        keep = jnp.where(col == k, ci - ri, col - k) >= 0
        q_ref[pl.ds(kk, NB), :NB] = jnp.where(keep, q[:, :NB], 0.0).astype(jnp.bfloat16)
        q_ref[pl.ds(kk, NB), NB:] = q[:, NB:].astype(jnp.bfloat16)

    def step(k, logs):
        kk = pl.multiple_of(k * NB, NB)
        left = ub_ref[:, pl.ds(kk, NB)]
        for t in range(STEPS):
            j = lax.rem(k + t, STEPS)
            jj = pl.multiple_of(j * NB, NB)
            low, high = jnp.minimum(k, j), jnp.maximum(k, j)
            pair = low // 2
            place = pair * STEPS - pair * (pair - 1) + high - 2 * pair
            upd = lax.dot_general(left, ub_ref[:, pl.ds(jj, NB)], (((0,), (0,)), ((), ())), preferred_element_type=jnp.float32)
            w_ref[:, t * NB:(t + 1) * NB] = d_ref[lax.rem(low, 2), place] - upd
        w_ref[:, STEPS * NB:] = eye
        if not isinstance(k, int):
            columns(k - 1)
        wide = (0, STEPS)
        for s in range(NB // SB):
            r0 = s * SB
            nb = SB // 8
            R = [[w_ref[r0 + 8 * b:r0 + 8 * b + 8, t * NB:(t + 1) * NB] for b in range(nb)] for t in wide]
            cols = [{b: jnp.broadcast_to(R[0][b][:, r0 + q:r0 + q + 1], (8, NB)) for b in range(q // 8, nb)} for q in range(SB)]
            for p in range(SB):
                pb, pr = p // 8, p % 8
                inv = lax.rsqrt(jnp.broadcast_to(cols[p][pb][pr:pr + 1, :], (8, NB)))
                l = {b: cols[p][b] * inv for b in range(pb, nb)}
                for q in range(p + 1, SB):
                    m = jnp.broadcast_to(l[q // 8][q % 8:q % 8 + 1, :], (8, NB))
                    for b in range(q // 8, nb):
                        cols[q][b] = cols[q][b] - l[b] * m
                for t in range(2):
                    u = jnp.broadcast_to(R[t][pb][pr:pr + 1, :], (8, NB)) * inv
                    if pr < 7:
                        R[t][pb] = jnp.where(rows8 == pr, u, R[t][pb] - jnp.where(rows8 > pr, l[pb], 0.0) * u)
                    else:
                        R[t][pb] = jnp.where(rows8 == pr, u, R[t][pb])
                    for b in range(pb + 1, nb):
                        R[t][b] = R[t][b] - l[b] * u
            R = [jnp.concatenate(x, axis=0) for x in R]
            for t in range(2):
                w_ref[r0:r0 + SB, wide[t] * NB:(wide[t] + 1) * NB] = R[t]
            if s < NB // SB - 1:
                X = jnp.concatenate(R, axis=1)
                xhi, xlo = split2(X)
                r1 = r0 + SB
                lh, ll = xhi[:, :NB], xlo[:, :NB]
                L = jnp.concatenate([lh, lh, ll], axis=0).T
                Rr = jnp.concatenate([xhi, xlo, xhi], axis=0)
                cuts = [(r1, NB)]
                for lo_, hi_ in cuts:
                    if lo_ < hi_:
                        upd = jnp.dot(L[lo_:hi_], Rr, preferred_element_type=jnp.float32)
                        for t in range(2):
                            sl = slice(wide[t] * NB, (wide[t] + 1) * NB)
                            w_ref[lo_:hi_, sl] = w_ref[lo_:hi_, sl] - upd[:, t * NB:(t + 1) * NB]
        lhi, llo = split2(w_ref[:, STEPS * NB:])
        shi, slo = split2(w_ref[:, NB:STEPS * NB])
        w_ref[:, NB:STEPS * NB] = jnp.dot(jnp.concatenate([lhi, lhi, llo], axis=1), jnp.concatenate([shi, slo, shi], axis=0), preferred_element_type=jnp.float32)
        tri = lax.broadcasted_iota(jnp.int32, (NB, NB), 0) <= lax.broadcasted_iota(jnp.int32, (NB, NB), 1)
        for t in range(STEPS):
            j = lax.rem(k + t, STEPS)
            jj = pl.multiple_of(j * NB, NB)
            keep = k + t < STEPS
            x = w_ref[:, t * NB:(t + 1) * NB]
            if t == 0:
                x = jnp.where(tri, x, 0.0)
                logs = logs + jnp.sum(jnp.log(jnp.sum(x * eye, axis=0, keepdims=True)), axis=1, keepdims=True)
            else:
                x = jnp.where(keep, x, 0.0)
            ub_ref[pl.ds(kk, NB), pl.ds(jj, NB)] = x.astype(jnp.bfloat16)
        linv_ref[k] = w_ref[:, STEPS * NB:]
        return logs

    logs = step(0, jnp.zeros((1, 1), jnp.float32))
    tops.wait()
    logs = lax.fori_loop(1, STEPS, step, logs)
    columns(STEPS - 1)
    logdet_ref[...] = logs * (2.0 / (STEPS * NB))

def chain(place, mine, other, top):
    return pl.pallas_call(
        chain_kernel,
        out_shape=(jax.ShapeDtypeStruct((STEPS * NB, STEPS * NB), jnp.bfloat16),
                   jax.ShapeDtypeStruct((STEPS, NB, NB), jnp.float32),
                   jax.ShapeDtypeStruct((STEPS * NB, LT * NB), jnp.bfloat16),
                   jax.ShapeDtypeStruct((1, 1), jnp.float32)),
        in_specs=[pl.BlockSpec(memory_space=pltpu.SMEM)] + [pl.BlockSpec(memory_space=pltpu.VMEM)] * 2 + [pl.BlockSpec(memory_space=pltpu.HBM)],
        out_specs=(pl.BlockSpec(memory_space=pltpu.VMEM),) * 4,
        scratch_shapes=[pltpu.VMEM((NB, (STEPS + 1) * NB), jnp.float32), pltpu.VMEM((2, HALF, NB, NB), jnp.float32),
                        pltpu.VMEM((STEPS, LT, NB, NB), jnp.float32), pltpu.SemaphoreType.DMA],
        compiler_params=pltpu.CompilerParams(vmem_limit_bytes=50 * 2**20),
        cost_estimate=pl.CostEstimate(flops=30_000_000_000, bytes_accessed=4 * 2**20, transcendentals=0),
        name="chain",
    )(place, mine, other, top)


def finish_kernel(place_ref, a_hbm, rp_ref, q_ref, ub_ref, linv_ref, pf_hbm, tr_hbm, a_ref, p_ref, b_ref, in_sem, p_sem, t_sem):
    row = place_ref[0]
    pairs = LT // 2
    loads = [pltpu.make_async_copy(a_hbm.at[:, pl.ds(2 * n, 2)], a_ref.at[n], in_sem.at[n]) for n in range(pairs)]
    for copy in loads:
        copy.start()
    ri = lax.broadcasted_iota(jnp.int32, (NB, NB), 0)
    ci = lax.broadcasted_iota(jnp.int32, (NB, NB), 1)
    scale = jnp.exp2(rp_ref[:, STEPS * LT * 8:STEPS * LT * 8 + 8] - SHIFT).reshape(NB, NB)
    stores = []
    later = None
    for k in range(STEPS):
        lhi, llo = split2(linv_ref[k])
        tiles = [rp_ref[:, (k * LT + l) * 8:(k * LT + l + 1) * 8].reshape(NB, NB) * scale for l in range(LT)]
        s = jnp.concatenate(tiles, axis=0)
        if k % 2 == 0:
            if k:
                both = jnp.dot(b_ref[:, :k * NB], ub_ref[:k * NB, k * NB:(k + 2) * NB], preferred_element_type=jnp.float32)
                s = s - both[:, :NB]
                later = both[:, NB:]
        else:
            s = s - jnp.dot(b_ref[:, (k - 1) * NB:k * NB], ub_ref[(k - 1) * NB:k * NB, k * NB:(k + 1) * NB],
                            preferred_element_type=jnp.float32)
            if k > 1:
                s = s - later
        shi, slo = split2(s)
        zero = jnp.zeros_like(llo)
        weights = jnp.concatenate([jnp.concatenate([lhi, lhi], axis=1), jnp.concatenate([llo, zero], axis=1)], axis=0)
        p = lax.dot_general(jnp.concatenate([shi, slo], axis=1), weights, (((1,), (1,)), ((), ())),
                            preferred_element_type=jnp.float32)
        p = p[:, :NB] + p[:, NB:]
        keep = jnp.where(row == k, ri - ci, row - k) >= 0
        first = jnp.where(keep, p[:NB], 0.0)
        p_ref[0, k] = first
        for l in range(1, LT):
            p_ref[l, k] = p[l * NB:(l + 1) * NB]
        b_ref[:NB, k * NB:(k + 1) * NB] = first.astype(jnp.bfloat16)
        b_ref[NB:, k * NB:(k + 1) * NB] = p[NB:].astype(jnp.bfloat16)
        store = pltpu.make_async_copy(p_ref.at[:, k], pf_hbm.at[:, k], p_sem.at[k])
        store.start()
        stores.append(store)
        if k % 2 == 0:
            continue
        for n in range(pairs):
            if k == 1:
                loads[n].wait()
            upd = jnp.dot(b_ref[:, (k - 1) * NB:(k + 1) * NB], q_ref[(k - 1) * NB:(k + 1) * NB, 2 * n * NB:2 * (n + 1) * NB],
                          preferred_element_type=jnp.float32)
            for l in range(LT):
                for m in range(2):
                    a_ref[n, l, m] = a_ref[n, l, m] - upd[l * NB:(l + 1) * NB, m * NB:(m + 1) * NB]
            if k == STEPS - 1:
                store = pltpu.make_async_copy(a_ref.at[n], tr_hbm.at[:, pl.ds(2 * n, 2)], t_sem.at[n])
                store.start()
                stores.append(store)
    for store in stores:
        store.wait()


def finish(place, a, rp, q, ub, linv):
    vm = pl.BlockSpec(memory_space=pltpu.VMEM)
    hb = pl.BlockSpec(memory_space=pltpu.HBM)
    return pl.pallas_call(
        finish_kernel,
        out_shape=(jax.ShapeDtypeStruct((LT, STEPS, NB, NB), jnp.float32),
                   jax.ShapeDtypeStruct((LT, LT, NB, NB), jnp.float32)),
        in_specs=[pl.BlockSpec(memory_space=pltpu.SMEM), hb, vm, vm, vm, vm],
        out_specs=(hb, hb),
        scratch_shapes=[pltpu.VMEM((LT // 2, LT, 2, NB, NB), jnp.float32), pltpu.VMEM((LT, STEPS, NB, NB), jnp.float32),
                        pltpu.VMEM((LT * NB, STEPS * NB), jnp.bfloat16), pltpu.SemaphoreType.DMA((LT // 2,)),
                        pltpu.SemaphoreType.DMA((STEPS,)), pltpu.SemaphoreType.DMA((LT // 2,))],
        compiler_params=pltpu.CompilerParams(vmem_limit_bytes=44 * 2**20),
        cost_estimate=pl.CostEstimate(flops=4_000_000_000, bytes_accessed=14 * 2**20, transcendentals=0),
        name="finish",
    )(place, a, rp, q, ub, linv)


def spread_kernel(x_ref, o_ref):
    tiles = [x_ref[p, q] for p in range(STEPS // 2) for q in range(2 * p, STEPS)]
    for j in range(16):
        for n, tile in enumerate(tiles):
            o_ref[j, n] = tile


def spread_half(x):
    return pl.pallas_call(
        spread_kernel,
        out_shape=jax.ShapeDtypeStruct((16, HALF, 8, NB), jnp.float32),
        in_specs=[pl.BlockSpec(memory_space=pltpu.VMEM)],
        out_specs=pl.BlockSpec(memory_space=pltpu.VMEM),
        compiler_params=pltpu.CompilerParams(vmem_limit_bytes=4 * 2**20),
        name="spread",
    )(x)


def packed(x):
    top = jnp.maximum(jnp.max(jnp.abs(x)), 1e-30)
    power = jnp.floor(jnp.log2(top))
    body = (x * jnp.exp2(SHIFT - power)).astype(jnp.float16)
    return jnp.concatenate([body, jnp.full((16, NB), power, jnp.float16)], axis=0)


def shards(covariance):
    matrix = covariance[:, 0, :, 0]
    row = lax.axis_index("row")
    place = jnp.stack([row, lax.axis_index("col")]).astype(jnp.int32)
    across = lax.all_gather(matrix[0], "row", axis=0, tiled=False)
    first = matrix[:, 0].reshape(LT, 16, 8, NB).transpose(1, 0, 2, 3).reshape(16 * LT * 8, NB)
    slabs = lax.all_to_all(first, "col", 0, 0, tiled=True).reshape(16, LT, 8, NB)[:STEPS]
    sent = jnp.broadcast_to(slabs[None, :, 0], (8, STEPS, 8, NB))
    sent, slabs = lax.optimization_barrier((sent, slabs))
    groups = [[2 * z + c for z in range(8)] for c in range(2)]
    lead = lax.all_to_all(sent, "row", 0, 0, tiled=True, axis_index_groups=groups)
    half = packed(slabs.reshape(STEPS * LT * 8, NB))
    half, lead = lax.optimization_barrier((jnp.broadcast_to(half[None], (16,) + half.shape), spread_half(lead)))
    mine = lax.all_to_all(lead, "col", 0, 0, tiled=True)
    half, mine = lax.optimization_barrier((half, mine))
    other = lax.ppermute(mine, "row", [(i, i ^ 1) for i in range(16)])
    down = lax.all_to_all(half, "col", 0, 0, tiled=True)
    ub, linv, q, logdet = chain(place, mine, other, across)
    down, q = lax.optimization_barrier((down, q))
    panel, trailing = finish(place, matrix, down.astype(jnp.float32), q, ub, linv)
    return panel[:, None], trailing[:, None, :, None], logdet[0, 0]


def solution(mesh):
    in_specs = (P(None, "row", None, "col", None, None),)
    out_specs = (P(None, "row", None, None, None), P(None, "row", None, "col", None, None), P())
    return jax.shard_map(shards, mesh=mesh, in_specs=in_specs, out_specs=out_specs, check_vma=False)
```

```python
import jax
import jax.numpy as jnp
from jax import lax
from jax.experimental import pallas as pl
from jax.experimental.pallas import tpu as pltpu
from jax.sharding import PartitionSpec as P

STEPS = 6
NB = 128
LT = 8
SB = 32
HALF = 12
SHIFT = 13.0


def split2(x):
    hi = x.astype(jnp.bfloat16)
    lo = (x - hi.astype(jnp.float32)).astype(jnp.bfloat16)
    return hi, lo

def chain_kernel(place_ref, mine_ref, other_ref, top_hbm, ub_ref, linv_ref, q_ref, logdet_ref, w_ref, d_ref, top_ref, sem):
    tops = pltpu.make_async_copy(top_hbm.at[pl.ds(0, STEPS)], top_ref, sem)
    tops.start()
    col = place_ref[1]
    core = lax.rem(place_ref[0], 2)
    for n in range(HALF):
        d_ref[core, n] = mine_ref[:, n].reshape(NB, NB)
        d_ref[1 - core, n] = other_ref[:, n].reshape(NB, NB)
    ub_ref[...] = jnp.zeros_like(ub_ref)
    q_ref[...] = jnp.zeros_like(q_ref)
    eye = (lax.broadcasted_iota(jnp.int32, (NB, NB), 0) == lax.broadcasted_iota(jnp.int32, (NB, NB), 1)).astype(jnp.float32)
    rows8 = lax.broadcasted_iota(jnp.int32, (8, NB), 0)
    ri = lax.broadcasted_iota(jnp.int32, (NB, NB), 0)
    ci = lax.broadcasted_iota(jnp.int32, (NB, NB), 1)

    def columns(k):
        kk = pl.multiple_of(k * NB, NB)
        lhi, llo = split2(linv_ref[k])
        x = jnp.concatenate([top_ref[k, m] for m in range(LT)], axis=1)
        x = x - lax.dot_general(ub_ref[:, pl.ds(kk, NB)], q_ref[...], (((0,), (0,)), ((), ())),
                                preferred_element_type=jnp.float32)
        xhi, xlo = split2(x)
        q = jnp.dot(jnp.concatenate([lhi, lhi, llo], axis=1), jnp.concatenate([xhi, xlo, xhi], axis=0),
                    preferred_element_type=jnp.float32)
        keep = jnp.where(col == k, ci - ri, col - k) >= 0
        q_ref[pl.ds(kk, NB), :NB] = jnp.where(keep, q[:, :NB], 0.0).astype(jnp.bfloat16)
        q_ref[pl.ds(kk, NB), NB:] = q[:, NB:].astype(jnp.bfloat16)

    def step(k, logs):
        kk = pl.multiple_of(k * NB, NB)
        left = ub_ref[:, pl.ds(kk, NB)]
        for t in range(STEPS):
            j = lax.rem(k + t, STEPS)
            jj = pl.multiple_of(j * NB, NB)
            low, high = jnp.minimum(k, j), jnp.maximum(k, j)
            pair = low // 2
            place = pair * STEPS - pair * (pair - 1) + high - 2 * pair
            upd = lax.dot_general(left, ub_ref[:, pl.ds(jj, NB)], (((0,), (0,)), ((), ())), preferred_element_type=jnp.float32)
            w_ref[:, t * NB:(t + 1) * NB] = d_ref[lax.rem(low, 2), place] - upd
        w_ref[:, STEPS * NB:] = eye
        if not isinstance(k, int):
            columns(k - 1)
        wide = (0, STEPS)
        for s in range(NB // SB):
            r0 = s * SB
            nb = SB // 8
            R = [[w_ref[r0 + 8 * b:r0 + 8 * b + 8, t * NB:(t + 1) * NB] for b in range(nb)] for t in wide]
            cols = [{b: jnp.broadcast_to(R[0][b][:, r0 + q:r0 + q + 1], (8, NB)) for b in range(q // 8, nb)} for q in range(SB)]
            for p in range(0, SB, 4):
                pb, pr = p // 8, p % 8
                c = [[None] * 4 for _ in range(4)]
                for i in range(4):
                    for j in range(i + 1):
                        c[i][j] = jnp.broadcast_to(cols[p + j][pb][pr + i:pr + i + 1, :], (8, NB))
                inv = [None] * 4
                l = [None] * 4
                for j in range(4):
                    inv[j] = lax.rsqrt(c[j][j])
                    for i in range(j + 1, 4):
                        c[i][j] = c[i][j] * inv[j]
                    for i in range(j + 1, 4):
                        for m in range(j + 1, i + 1):
                            c[i][m] = c[i][m] - c[i][j] * c[m][j]
                    x = {b: cols[p + j][b] for b in range(pb, nb)}
                    for m in range(j):
                        x = {b: x[b] - l[m][b] * c[j][m] for b in x}
                    l[j] = {b: x[b] * inv[j] for b in x}
                for q in range(p + 4, SB):
                    for j in range(4):
                        m = jnp.broadcast_to(l[j][q // 8][q % 8:q % 8 + 1, :], (8, NB))
                        for b in range(q // 8, nb):
                            cols[q][b] = cols[q][b] - l[j][b] * m
                for t in range(2):
                    u = []
                    for j in range(4):
                        x = jnp.broadcast_to(R[t][pb][pr + j:pr + j + 1, :], (8, NB))
                        for m in range(j):
                            x = x - c[j][m] * u[m]
                        u.append(x * inv[j])
                    own = R[t][pb]
                    if pr + 4 < 8:
                        for j in range(4):
                            own = own - jnp.where(rows8 >= pr + 4, l[j][pb], 0.0) * u[j]
                    for j in range(4):
                        own = jnp.where(rows8 == pr + j, u[j], own)
                    R[t][pb] = own
                    for b in range(pb + 1, nb):
                        for j in range(4):
                            R[t][b] = R[t][b] - l[j][b] * u[j]
            R = [jnp.concatenate(x, axis=0) for x in R]
            for t in range(2):
                w_ref[r0:r0 + SB, wide[t] * NB:(wide[t] + 1) * NB] = R[t]
            if s < NB // SB - 1:
                X = jnp.concatenate(R, axis=1)
                xhi, xlo = split2(X)
                r1 = r0 + SB
                lh, ll = xhi[:, :NB], xlo[:, :NB]
                L = jnp.concatenate([lh, lh, ll], axis=0).T
                Rr = jnp.concatenate([xhi, xlo, xhi], axis=0)
                cuts = [(r1, NB)]
                for lo_, hi_ in cuts:
                    if lo_ < hi_:
                        upd = jnp.dot(L[lo_:hi_], Rr, preferred_element_type=jnp.float32)
                        for t in range(2):
                            sl = slice(wide[t] * NB, (wide[t] + 1) * NB)
                            w_ref[lo_:hi_, sl] = w_ref[lo_:hi_, sl] - upd[:, t * NB:(t + 1) * NB]
        lhi, llo = split2(w_ref[:, STEPS * NB:])
        shi, slo = split2(w_ref[:, NB:STEPS * NB])
        w_ref[:, NB:STEPS * NB] = jnp.dot(jnp.concatenate([lhi, lhi, llo], axis=1), jnp.concatenate([shi, slo, shi], axis=0), preferred_element_type=jnp.float32)
        tri = lax.broadcasted_iota(jnp.int32, (NB, NB), 0) <= lax.broadcasted_iota(jnp.int32, (NB, NB), 1)
        for t in range(STEPS):
            j = lax.rem(k + t, STEPS)
            jj = pl.multiple_of(j * NB, NB)
            keep = k + t < STEPS
            x = w_ref[:, t * NB:(t + 1) * NB]
            if t == 0:
                x = jnp.where(tri, x, 0.0)
                logs = logs + jnp.sum(jnp.log(jnp.sum(x * eye, axis=0, keepdims=True)), axis=1, keepdims=True)
            else:
                x = jnp.where(keep, x, 0.0)
            ub_ref[pl.ds(kk, NB), pl.ds(jj, NB)] = x.astype(jnp.bfloat16)
        linv_ref[k] = w_ref[:, STEPS * NB:]
        return logs

    logs = step(0, jnp.zeros((1, 1), jnp.float32))
    tops.wait()
    logs = lax.fori_loop(1, STEPS, step, logs)
    columns(STEPS - 1)
    logdet_ref[...] = logs * (2.0 / (STEPS * NB))

def chain(place, mine, other, top):
    return pl.pallas_call(
        chain_kernel,
        out_shape=(jax.ShapeDtypeStruct((STEPS * NB, STEPS * NB), jnp.bfloat16),
                   jax.ShapeDtypeStruct((STEPS, NB, NB), jnp.float32),
                   jax.ShapeDtypeStruct((STEPS * NB, LT * NB), jnp.bfloat16),
                   jax.ShapeDtypeStruct((1, 1), jnp.float32)),
        in_specs=[pl.BlockSpec(memory_space=pltpu.SMEM)] + [pl.BlockSpec(memory_space=pltpu.VMEM)] * 2 + [pl.BlockSpec(memory_space=pltpu.HBM)],
        out_specs=(pl.BlockSpec(memory_space=pltpu.VMEM),) * 4,
        scratch_shapes=[pltpu.VMEM((NB, (STEPS + 1) * NB), jnp.float32), pltpu.VMEM((2, HALF, NB, NB), jnp.float32),
                        pltpu.VMEM((STEPS, LT, NB, NB), jnp.float32), pltpu.SemaphoreType.DMA],
        compiler_params=pltpu.CompilerParams(vmem_limit_bytes=50 * 2**20),
        cost_estimate=pl.CostEstimate(flops=30_000_000_000, bytes_accessed=4 * 2**20, transcendentals=0),
        name="chain",
    )(place, mine, other, top)


def finish_kernel(place_ref, a_hbm, rp_ref, q_ref, ub_ref, linv_ref, pf_hbm, tr_hbm, a_ref, p_ref, b_ref, in_sem, p_sem, t_sem):
    row = place_ref[0]
    pairs = LT // 2
    loads = [pltpu.make_async_copy(a_hbm.at[:, pl.ds(2 * n, 2)], a_ref.at[n], in_sem.at[n]) for n in range(pairs)]
    for copy in loads:
        copy.start()
    ri = lax.broadcasted_iota(jnp.int32, (NB, NB), 0)
    ci = lax.broadcasted_iota(jnp.int32, (NB, NB), 1)
    scale = jnp.exp2(rp_ref[:, STEPS * LT * 8:STEPS * LT * 8 + 8] - SHIFT).reshape(NB, NB)
    stores = []
    later = None
    for k in range(STEPS):
        lhi, llo = split2(linv_ref[k])
        tiles = [rp_ref[:, (k * LT + l) * 8:(k * LT + l + 1) * 8].reshape(NB, NB) * scale for l in range(LT)]
        s = jnp.concatenate(tiles, axis=0)
        if k % 2 == 0:
            if k:
                both = jnp.dot(b_ref[:, :k * NB], ub_ref[:k * NB, k * NB:(k + 2) * NB], preferred_element_type=jnp.float32)
                s = s - both[:, :NB]
                later = both[:, NB:]
        else:
            s = s - jnp.dot(b_ref[:, (k - 1) * NB:k * NB], ub_ref[(k - 1) * NB:k * NB, k * NB:(k + 1) * NB],
                            preferred_element_type=jnp.float32)
            if k > 1:
                s = s - later
        shi, slo = split2(s)
        zero = jnp.zeros_like(llo)
        weights = jnp.concatenate([jnp.concatenate([lhi, lhi], axis=1), jnp.concatenate([llo, zero], axis=1)], axis=0)
        p = lax.dot_general(jnp.concatenate([shi, slo], axis=1), weights, (((1,), (1,)), ((), ())),
                            preferred_element_type=jnp.float32)
        p = p[:, :NB] + p[:, NB:]
        keep = jnp.where(row == k, ri - ci, row - k) >= 0
        first = jnp.where(keep, p[:NB], 0.0)
        p_ref[0, k] = first
        for l in range(1, LT):
            p_ref[l, k] = p[l * NB:(l + 1) * NB]
        b_ref[:NB, k * NB:(k + 1) * NB] = first.astype(jnp.bfloat16)
        b_ref[NB:, k * NB:(k + 1) * NB] = p[NB:].astype(jnp.bfloat16)
        store = pltpu.make_async_copy(p_ref.at[:, k], pf_hbm.at[:, k], p_sem.at[k])
        store.start()
        stores.append(store)
        if k % 2 == 0:
            continue
        for n in range(pairs):
            if k == 1:
                loads[n].wait()
            upd = jnp.dot(b_ref[:, (k - 1) * NB:(k + 1) * NB], q_ref[(k - 1) * NB:(k + 1) * NB, 2 * n * NB:2 * (n + 1) * NB],
                          preferred_element_type=jnp.float32)
            for l in range(LT):
                for m in range(2):
                    a_ref[n, l, m] = a_ref[n, l, m] - upd[l * NB:(l + 1) * NB, m * NB:(m + 1) * NB]
            if k == STEPS - 1:
                store = pltpu.make_async_copy(a_ref.at[n], tr_hbm.at[:, pl.ds(2 * n, 2)], t_sem.at[n])
                store.start()
                stores.append(store)
    for store in stores:
        store.wait()


def finish(place, a, rp, q, ub, linv):
    vm = pl.BlockSpec(memory_space=pltpu.VMEM)
    hb = pl.BlockSpec(memory_space=pltpu.HBM)
    return pl.pallas_call(
        finish_kernel,
        out_shape=(jax.ShapeDtypeStruct((LT, STEPS, NB, NB), jnp.float32),
                   jax.ShapeDtypeStruct((LT, LT, NB, NB), jnp.float32)),
        in_specs=[pl.BlockSpec(memory_space=pltpu.SMEM), hb, vm, vm, vm, vm],
        out_specs=(hb, hb),
        scratch_shapes=[pltpu.VMEM((LT // 2, LT, 2, NB, NB), jnp.float32), pltpu.VMEM((LT, STEPS, NB, NB), jnp.float32),
                        pltpu.VMEM((LT * NB, STEPS * NB), jnp.bfloat16), pltpu.SemaphoreType.DMA((LT // 2,)),
                        pltpu.SemaphoreType.DMA((STEPS,)), pltpu.SemaphoreType.DMA((LT // 2,))],
        compiler_params=pltpu.CompilerParams(vmem_limit_bytes=44 * 2**20),
        cost_estimate=pl.CostEstimate(flops=4_000_000_000, bytes_accessed=14 * 2**20, transcendentals=0),
        name="finish",
    )(place, a, rp, q, ub, linv)


def spread_kernel(x_ref, o_ref):
    tiles = [x_ref[p, q] for p in range(STEPS // 2) for q in range(2 * p, STEPS)]
    for j in range(16):
        for n, tile in enumerate(tiles):
            o_ref[j, n] = tile


def spread_half(x):
    return pl.pallas_call(
        spread_kernel,
        out_shape=jax.ShapeDtypeStruct((16, HALF, 8, NB), jnp.float32),
        in_specs=[pl.BlockSpec(memory_space=pltpu.VMEM)],
        out_specs=pl.BlockSpec(memory_space=pltpu.VMEM),
        compiler_params=pltpu.CompilerParams(vmem_limit_bytes=4 * 2**20),
        name="spread",
    )(x)


def packed(x):
    top = jnp.maximum(jnp.max(jnp.abs(x)), 1e-30)
    power = jnp.floor(jnp.log2(top))
    body = (x * jnp.exp2(SHIFT - power)).astype(jnp.float16)
    return jnp.concatenate([body, jnp.full((8, NB), power, jnp.float16)], axis=0)


def shards(covariance):
    matrix = covariance[:, 0, :, 0]
    row = lax.axis_index("row")
    place = jnp.stack([row, lax.axis_index("col")]).astype(jnp.int32)
    across = lax.all_gather(matrix[0], "row", axis=0, tiled=False)
    first = matrix[:, 0].reshape(LT, 16, 8, NB).transpose(1, 0, 2, 3).reshape(16 * LT * 8, NB)
    slabs = lax.all_to_all(first, "col", 0, 0, tiled=True).reshape(16, LT, 8, NB)[:STEPS]
    sent = jnp.broadcast_to(slabs[None, :, 0], (8, STEPS, 8, NB))
    sent, slabs = lax.optimization_barrier((sent, slabs))
    groups = [[2 * z + c for z in range(8)] for c in range(2)]
    lead = lax.all_to_all(sent, "row", 0, 0, tiled=True, axis_index_groups=groups)
    half = packed(slabs.reshape(STEPS * LT * 8, NB))
    half, lead = lax.optimization_barrier((jnp.broadcast_to(half[None], (16,) + half.shape), spread_half(lead)))
    mine = lax.all_to_all(lead, "col", 0, 0, tiled=True)
    half, mine = lax.optimization_barrier((half, mine))
    other = lax.ppermute(mine, "row", [(i, i ^ 1) for i in range(16)])
    down = lax.all_to_all(half, "col", 0, 0, tiled=True)
    ub, linv, q, logdet = chain(place, mine, other, across)
    down, q = lax.optimization_barrier((down, q))
    panel, trailing = finish(place, matrix, down.astype(jnp.float32), q, ub, linv)
    return panel[:, None], trailing[:, None, :, None], logdet[0, 0]


def solution(mesh):
    in_specs = (P(None, "row", None, "col", None, None),)
    out_specs = (P(None, "row", None, None, None), P(None, "row", None, "col", None, None), P())
    return jax.shard_map(shards, mesh=mesh, in_specs=in_specs, out_specs=out_specs, check_vma=False)
```

```python
import jax
import jax.numpy as jnp
from jax import lax
from jax.experimental import pallas as pl
from jax.experimental.pallas import tpu as pltpu
from jax.sharding import PartitionSpec as P

STEPS = 6
NB = 128
LT = 8
SB = 32
HALF = 12
SHIFT = 13.0


def split2(x):
    hi = x.astype(jnp.bfloat16)
    lo = (x - hi.astype(jnp.float32)).astype(jnp.bfloat16)
    return hi, lo

def chain_kernel(place_ref, mine_ref, other_ref, top_hbm, ub_ref, linv_ref, q_ref, logdet_ref, w_ref, d_ref, top_ref, sem):
    tops = pltpu.make_async_copy(top_hbm.at[pl.ds(0, STEPS)], top_ref, sem)
    tops.start()
    col = place_ref[1]
    core = lax.rem(place_ref[0], 2)
    for n in range(HALF):
        d_ref[core, n] = mine_ref[:, n].reshape(NB, NB)
        d_ref[1 - core, n] = other_ref[:, n].reshape(NB, NB)
    ub_ref[...] = jnp.zeros_like(ub_ref)
    q_ref[...] = jnp.zeros_like(q_ref)
    eye = (lax.broadcasted_iota(jnp.int32, (NB, NB), 0) == lax.broadcasted_iota(jnp.int32, (NB, NB), 1)).astype(jnp.float32)
    rows8 = lax.broadcasted_iota(jnp.int32, (8, NB), 0)
    ri = lax.broadcasted_iota(jnp.int32, (NB, NB), 0)
    ci = lax.broadcasted_iota(jnp.int32, (NB, NB), 1)

    def columns(k):
        kk = pl.multiple_of(k * NB, NB)
        lhi, llo = split2(linv_ref[k])
        x = jnp.concatenate([top_ref[k, m] for m in range(LT)], axis=1)
        x = x - lax.dot_general(ub_ref[:, pl.ds(kk, NB)], q_ref[...], (((0,), (0,)), ((), ())),
                                preferred_element_type=jnp.float32)
        xhi, xlo = split2(x)
        q = jnp.dot(jnp.concatenate([lhi, lhi, llo], axis=1), jnp.concatenate([xhi, xlo, xhi], axis=0),
                    preferred_element_type=jnp.float32)
        keep = jnp.where(col == k, ci - ri, col - k) >= 0
        q_ref[pl.ds(kk, NB), :NB] = jnp.where(keep, q[:, :NB], 0.0).astype(jnp.bfloat16)
        q_ref[pl.ds(kk, NB), NB:] = q[:, NB:].astype(jnp.bfloat16)

    def step(k, logs):
        kk = pl.multiple_of(k * NB, NB)
        left = ub_ref[:, pl.ds(kk, NB)]
        for t in range(STEPS):
            j = lax.rem(k + t, STEPS)
            jj = pl.multiple_of(j * NB, NB)
            low, high = jnp.minimum(k, j), jnp.maximum(k, j)
            pair = low // 2
            place = pair * STEPS - pair * (pair - 1) + high - 2 * pair
            upd = lax.dot_general(left, ub_ref[:, pl.ds(jj, NB)], (((0,), (0,)), ((), ())), preferred_element_type=jnp.float32)
            w_ref[:, t * NB:(t + 1) * NB] = d_ref[lax.rem(low, 2), place] - upd
        w_ref[:, STEPS * NB:] = eye
        if not isinstance(k, int):
            columns(k - 1)
        wide = (0, STEPS)
        for s in range(NB // SB):
            r0 = s * SB
            nb = SB // 8
            R = [[w_ref[r0 + 8 * b:r0 + 8 * b + 8, t * NB:(t + 1) * NB] for b in range(nb)] for t in wide]
            cols = [{b: jnp.broadcast_to(R[0][b][:, r0 + q:r0 + q + 1], (8, NB)) for b in range(q // 8, nb)} for q in range(SB)]
            for p in range(SB):
                pb, pr = p // 8, p % 8
                inv = lax.rsqrt(jnp.broadcast_to(cols[p][pb][pr:pr + 1, :], (8, NB)))
                l = {b: cols[p][b] * inv for b in range(pb, nb)}
                for q in range(p + 1, SB):
                    m = jnp.broadcast_to(l[q // 8][q % 8:q % 8 + 1, :], (8, NB))
                    for b in range(q // 8, nb):
                        cols[q][b] = cols[q][b] - l[b] * m
                for t in range(2):
                    u = jnp.broadcast_to(R[t][pb][pr:pr + 1, :], (8, NB)) * inv
                    if pr < 7:
                        R[t][pb] = jnp.where(rows8 == pr, u, R[t][pb] - jnp.where(rows8 > pr, l[pb], 0.0) * u)
                    else:
                        R[t][pb] = jnp.where(rows8 == pr, u, R[t][pb])
                    for b in range(pb + 1, nb):
                        R[t][b] = R[t][b] - l[b] * u
            R = [jnp.concatenate(x, axis=0) for x in R]
            for t in range(2):
                w_ref[r0:r0 + SB, wide[t] * NB:(wide[t] + 1) * NB] = R[t]
            if s < NB // SB - 1:
                X = jnp.concatenate(R, axis=1)
                xhi, xlo = split2(X)
                r1 = r0 + SB
                lh, ll = xhi[:, :NB], xlo[:, :NB]
                L = jnp.concatenate([lh, lh, ll], axis=0).T
                Rr = jnp.concatenate([xhi, xlo, xhi], axis=0)
                cuts = [(r1, NB)]
                for lo_, hi_ in cuts:
                    if lo_ < hi_:
                        upd = jnp.dot(L[lo_:hi_], Rr, preferred_element_type=jnp.float32)
                        for t in range(2):
                            sl = slice(wide[t] * NB, (wide[t] + 1) * NB)
                            w_ref[lo_:hi_, sl] = w_ref[lo_:hi_, sl] - upd[:, t * NB:(t + 1) * NB]
        lhi, llo = split2(w_ref[:, STEPS * NB:])
        shi, slo = split2(w_ref[:, NB:STEPS * NB])
        w_ref[:, NB:STEPS * NB] = jnp.dot(jnp.concatenate([lhi, lhi, llo], axis=1), jnp.concatenate([shi, slo, shi], axis=0), preferred_element_type=jnp.float32)
        tri = lax.broadcasted_iota(jnp.int32, (NB, NB), 0) <= lax.broadcasted_iota(jnp.int32, (NB, NB), 1)
        for t in range(STEPS):
            j = lax.rem(k + t, STEPS)
            jj = pl.multiple_of(j * NB, NB)
            keep = k + t < STEPS
            x = w_ref[:, t * NB:(t + 1) * NB]
            if t == 0:
                x = jnp.where(tri, x, 0.0)
                logs = logs + jnp.sum(jnp.log(jnp.sum(x * eye, axis=0, keepdims=True)), axis=1, keepdims=True)
            else:
                x = jnp.where(keep, x, 0.0)
            ub_ref[pl.ds(kk, NB), pl.ds(jj, NB)] = x.astype(jnp.bfloat16)
        linv_ref[k] = w_ref[:, STEPS * NB:]
        return logs

    logs = step(0, jnp.zeros((1, 1), jnp.float32))
    tops.wait()
    logs = lax.fori_loop(1, STEPS, step, logs)
    columns(STEPS - 1)
    logdet_ref[...] = logs * (2.0 / (STEPS * NB))

def chain(place, mine, other, top):
    return pl.pallas_call(
        chain_kernel,
        out_shape=(jax.ShapeDtypeStruct((STEPS * NB, STEPS * NB), jnp.bfloat16),
                   jax.ShapeDtypeStruct((STEPS, NB, NB), jnp.float32),
                   jax.ShapeDtypeStruct((STEPS * NB, LT * NB), jnp.bfloat16),
                   jax.ShapeDtypeStruct((1, 1), jnp.float32)),
        in_specs=[pl.BlockSpec(memory_space=pltpu.SMEM)] + [pl.BlockSpec(memory_space=pltpu.VMEM)] * 2 + [pl.BlockSpec(memory_space=pltpu.HBM)],
        out_specs=(pl.BlockSpec(memory_space=pltpu.VMEM),) * 4,
        scratch_shapes=[pltpu.VMEM((NB, (STEPS + 1) * NB), jnp.float32), pltpu.VMEM((2, HALF, NB, NB), jnp.float32),
                        pltpu.VMEM((STEPS, LT, NB, NB), jnp.float32), pltpu.SemaphoreType.DMA],
        compiler_params=pltpu.CompilerParams(vmem_limit_bytes=47 * 2**20),
        cost_estimate=pl.CostEstimate(flops=30_000_000_000, bytes_accessed=4 * 2**20, transcendentals=0),
        name="chain",
    )(place, mine, other, top)


def finish_kernel(place_ref, a_ref, rp_ref, q_ref, ub_ref, linv_ref, pf_hbm, tr_hbm, t_ref, p_ref, b_ref, p_sem, t_sem):
    row = place_ref[0]
    pairs = LT // 2
    ri = lax.broadcasted_iota(jnp.int32, (NB, NB), 0)
    ci = lax.broadcasted_iota(jnp.int32, (NB, NB), 1)
    scale = jnp.exp2(rp_ref[:, STEPS * LT * 8:STEPS * LT * 8 + 8] - SHIFT).reshape(NB, NB)
    stores = []
    later = None
    for k in range(STEPS):
        lhi, llo = split2(linv_ref[k])
        tiles = [rp_ref[:, (k * LT + l) * 8:(k * LT + l + 1) * 8].reshape(NB, NB) * scale for l in range(LT)]
        s = jnp.concatenate(tiles, axis=0)
        if k % 2 == 0:
            if k:
                both = jnp.dot(b_ref[:, :k * NB], ub_ref[:k * NB, k * NB:(k + 2) * NB], preferred_element_type=jnp.float32)
                s = s - both[:, :NB]
                later = both[:, NB:]
        else:
            s = s - jnp.dot(b_ref[:, (k - 1) * NB:k * NB], ub_ref[(k - 1) * NB:k * NB, k * NB:(k + 1) * NB],
                            preferred_element_type=jnp.float32)
            if k > 1:
                s = s - later
        shi, slo = split2(s)
        zero = jnp.zeros_like(llo)
        weights = jnp.concatenate([jnp.concatenate([lhi, lhi], axis=1), jnp.concatenate([llo, zero], axis=1)], axis=0)
        p = lax.dot_general(jnp.concatenate([shi, slo], axis=1), weights, (((1,), (1,)), ((), ())),
                            preferred_element_type=jnp.float32)
        p = p[:, :NB] + p[:, NB:]
        keep = jnp.where(row == k, ri - ci, row - k) >= 0
        first = jnp.where(keep, p[:NB], 0.0)
        p_ref[0, k] = first
        for l in range(1, LT):
            p_ref[l, k] = p[l * NB:(l + 1) * NB]
        b_ref[:NB, k * NB:(k + 1) * NB] = first.astype(jnp.bfloat16)
        b_ref[NB:, k * NB:(k + 1) * NB] = p[NB:].astype(jnp.bfloat16)
        store = pltpu.make_async_copy(p_ref.at[:, k], pf_hbm.at[:, k], p_sem.at[k])
        store.start()
        stores.append(store)
        if k % 2 == 0:
            continue
        for n in range(pairs):
            upd = jnp.dot(b_ref[:, (k - 1) * NB:(k + 1) * NB], q_ref[(k - 1) * NB:(k + 1) * NB, 2 * n * NB:2 * (n + 1) * NB],
                          preferred_element_type=jnp.float32)
            for l in range(LT):
                for m in range(2):
                    before = a_ref[l, 2 * n + m] if k == 1 else t_ref[n, l, m]
                    t_ref[n, l, m] = before - upd[l * NB:(l + 1) * NB, m * NB:(m + 1) * NB]
            if k == STEPS - 1:
                store = pltpu.make_async_copy(t_ref.at[n], tr_hbm.at[:, pl.ds(2 * n, 2)], t_sem.at[n])
                store.start()
                stores.append(store)
    for store in stores:
        store.wait()


def finish(place, a, rp, q, ub, linv):
    vm = pl.BlockSpec(memory_space=pltpu.VMEM)
    hb = pl.BlockSpec(memory_space=pltpu.HBM)
    return pl.pallas_call(
        finish_kernel,
        out_shape=(jax.ShapeDtypeStruct((LT, STEPS, NB, NB), jnp.float32),
                   jax.ShapeDtypeStruct((LT, LT, NB, NB), jnp.float32)),
        in_specs=[pl.BlockSpec(memory_space=pltpu.SMEM), vm, vm, vm, vm, vm],
        out_specs=(hb, hb),
        scratch_shapes=[pltpu.VMEM((LT // 2, LT, 2, NB, NB), jnp.float32), pltpu.VMEM((LT, STEPS, NB, NB), jnp.float32),
                        pltpu.VMEM((LT * NB, STEPS * NB), jnp.bfloat16),
                        pltpu.SemaphoreType.DMA((STEPS,)), pltpu.SemaphoreType.DMA((LT // 2,))],
        compiler_params=pltpu.CompilerParams(vmem_limit_bytes=36 * 2**20),
        cost_estimate=pl.CostEstimate(flops=4_000_000_000, bytes_accessed=14 * 2**20, transcendentals=0),
        name="finish",
    )(place, a, rp, q, ub, linv)


def spread_kernel(x_ref, o_ref):
    tiles = [x_ref[p, q] for p in range(STEPS // 2) for q in range(2 * p, STEPS)]
    for j in range(16):
        for n, tile in enumerate(tiles):
            o_ref[j, n] = tile


def spread_half(x):
    return pl.pallas_call(
        spread_kernel,
        out_shape=jax.ShapeDtypeStruct((16, HALF, 8, NB), jnp.float32),
        in_specs=[pl.BlockSpec(memory_space=pltpu.VMEM)],
        out_specs=pl.BlockSpec(memory_space=pltpu.VMEM),
        compiler_params=pltpu.CompilerParams(vmem_limit_bytes=4 * 2**20),
        name="spread",
    )(x)


def packed(x):
    top = jnp.maximum(jnp.max(jnp.abs(x)), 1e-30)
    power = jnp.floor(jnp.log2(top))
    body = (x * jnp.exp2(SHIFT - power)).astype(jnp.float16)
    return jnp.concatenate([body, jnp.full((16, NB), power, jnp.float16)], axis=0)


def shards(covariance):
    matrix = covariance[:, 0, :, 0]
    row = lax.axis_index("row")
    place = jnp.stack([row, lax.axis_index("col")]).astype(jnp.int32)
    across = lax.all_gather(matrix[0], "row", axis=0, tiled=False)
    first = matrix[:, 0].reshape(LT, 16, 8, NB).transpose(1, 0, 2, 3).reshape(16 * LT * 8, NB)
    slabs = lax.all_to_all(first, "col", 0, 0, tiled=True).reshape(16, LT, 8, NB)[:STEPS]
    sent = jnp.broadcast_to(slabs[None, :, 0], (8, STEPS, 8, NB))
    sent, slabs = lax.optimization_barrier((sent, slabs))
    groups = [[2 * z + c for z in range(8)] for c in range(2)]
    lead = lax.all_to_all(sent, "row", 0, 0, tiled=True, axis_index_groups=groups)
    half = packed(slabs.reshape(STEPS * LT * 8, NB))
    half, lead = lax.optimization_barrier((jnp.broadcast_to(half[None], (16,) + half.shape), spread_half(lead)))
    mine = lax.all_to_all(lead, "col", 0, 0, tiled=True)
    half, mine = lax.optimization_barrier((half, mine))
    other = lax.ppermute(mine, "row", [(i, i ^ 1) for i in range(16)])
    down = lax.all_to_all(half, "col", 0, 0, tiled=True)
    ub, linv, q, logdet = chain(place, mine, other, across)
    down, q = lax.optimization_barrier((down, q))
    panel, trailing = finish(place, matrix, down.astype(jnp.float32), q, ub, linv)
    return panel[:, None], trailing[:, None, :, None], logdet[0, 0]


def solution(mesh):
    in_specs = (P(None, "row", None, "col", None, None),)
    out_specs = (P(None, "row", None, None, None), P(None, "row", None, "col", None, None), P())
    return jax.shard_map(shards, mesh=mesh, in_specs=in_specs, out_specs=out_specs, check_vma=False)
```
